512 devices in a mesh: dp: 8 (over x, core), tensor: 64 (over z, y).
Axes of the slice: x: 4, y: 8, z: 8, core: 2. Of those that a mesh axis runs over, the one named last changes fastest.
Arguments:
- tokens: bfloat16 [4096, 4096], P('dp', 'tensor'), may hold values from -8 to 8
- gain: float32 [4096], replicated, may hold values from 0.1 to 1.9
- cotangent: bfloat16 [4096, 4096], P('dp', 'tensor'), may hold values from -30 to 30, as said below
- gate_weight: bfloat16 [4096, 14336], P('dp', 'tensor'), may hold values from -0.09375 to 0.09375
- up_weight: bfloat16 [4096, 14336], P('dp', 'tensor'), may hold values from -0.09375 to 0.09375
- down_weight: bfloat16 [14336, 4096], P('tensor', 'dp'), may hold values from -0.046875 to 0.046875
Outputs:
- grad_down: float32 [14336, 4096], P('tensor', 'dp')
- grad_gain: float32 [4096], P('tensor')
The draws below stay inside these ranges and needn't reach their ends.
Inputs may be any that keep to these rules, and one draw needn't show every extreme that they name: Each sequence's cotangent has its own overall scale.
All inputs are finite; a program needn't handle non-finite values.
Results may differ from the reference program's by a relative error of at most 0.015.
Values may be sent and summed in bfloat16 or wider, within the bound.
No kernel may reach another device: no remote copies, remote signals or barrier semaphores. Data moves between devices by JAX's collectives and lax.ppermute only.
A program may use at most 64 MiB of HBM per device.

```python
import math
import jax
import jax.numpy as jnp
from jax import lax

MODEL_FEATURES = 4096
FF = 14336
SEQUENCE_LENGTH = 64
LOCAL_SEQUENCES = 8
SEQS = 64
TOKENS = 4096
N_DP = 8


def draw_tokens(key, part):
    key = jax.random.fold_in(key, 5)
    first, second, third = jax.random.split(key, 3)
    base = jnp.clip(jax.random.normal(first, (TOKENS, MODEL_FEATURES), jnp.float32), -5.0, 5.0)
    common = jnp.clip(jax.random.normal(second, (SEQS, MODEL_FEATURES), jnp.float32), -5.0, 5.0)
    weight = jax.random.uniform(third, (TOKENS,), jnp.float32, 0.4, 1.2)
    shared = jnp.repeat(common, SEQUENCE_LENGTH, axis=0)
    return (0.6 * base + 0.8 * weight[:, None] * shared).astype(jnp.bfloat16)


def draw_cotangent(key, part):
    key = jax.random.fold_in(key, 11)
    first, second, third, fourth = jax.random.split(key, 4)
    base = jnp.clip(jax.random.normal(first, (TOKENS, MODEL_FEATURES), jnp.float32), -6.0, 6.0)
    common = jnp.clip(jax.random.normal(third, (SEQS, MODEL_FEATURES), jnp.float32), -6.0, 6.0)
    weight = jax.random.uniform(fourth, (TOKENS,), jnp.float32, 0.7, 1.1)
    mixed = 0.5 * base + 0.85 * weight[:, None] * jnp.repeat(common, SEQUENCE_LENGTH, axis=0)
    order = jnp.arange(SEQS, dtype=jnp.int32)
    ladder = 0.05 * 40.0 ** ((order * 3 % 8).astype(jnp.float32) / 7.0)
    jitter = jax.random.uniform(second, (SEQS,), jnp.float32, 0.8, 1.25)
    row_scale = jnp.repeat(ladder * jitter, SEQUENCE_LENGTH)
    return (mixed * row_scale[:, None]).astype(jnp.bfloat16)


def block_levels(rng, extent, pieces, low, largest):
    def one(dim, parts):
        steps = jax.random.uniform(jax.random.fold_in(jax.random.fold_in(rng, 6), dim), (parts,), jnp.float32, low / len(pieces), largest / len(pieces))
        return jnp.repeat(jnp.exp(steps), extent[dim] // parts).reshape((-1,) + (1,) * (len(extent) - dim - 1))

    level = one(*pieces[0])
    for cut in pieces[1:]:
        level = level * one(*cut)
    return level


def normal_values(key, extent, scale, reach, pieces=(), kind=jnp.bfloat16):
    entries = jax.random.normal(key, extent, jnp.float32) * scale
    if len(pieces) > 0:
        entries = block_levels(key, extent, pieces, -0.22, 0.18) * entries
    return jnp.clip(entries, min=-reach, max=reach).astype(kind)


def setup_inputs(seed: int = 0) -> dict:
    key_list = jax.random.split(jax.random.key(seed), 7)
    tokens = draw_tokens(jax.random.fold_in(key_list[6], 71), 0)
    gain = jnp.clip(1.0 + 0.18 * jax.random.normal(key_list[1], (MODEL_FEATURES,), jnp.float32), 0.1, 1.9)
    cotangent = draw_cotangent(jax.random.fold_in(key_list[6], 71), 0)
    gate_weight = normal_values(key_list[3], (MODEL_FEATURES, FF), MODEL_FEATURES ** -0.5, 0.09375, ((0, 8), (1, 64)))
    up_weight = normal_values(key_list[4], (MODEL_FEATURES, FF), MODEL_FEATURES ** -0.5, 0.09375, ((0, 8), (1, 64)))
    down_weight = normal_values(key_list[5], (FF, MODEL_FEATURES), FF ** -0.5, 0.046875, ((0, 64), (1, 8)))
    return dict(tokens=tokens, gain=gain, cotangent=cotangent, gate_weight=gate_weight, up_weight=up_weight, down_weight=down_weight)


def reference(tokens, gain, cotangent, gate_weight, up_weight, down_weight):
    rows = LOCAL_SEQUENCES * SEQUENCE_LENGTH
    down_bound = 0.6 * math.sqrt(SEQUENCE_LENGTH * FF * MODEL_FEATURES)
    gain_bound = 0.5 * math.sqrt(SEQUENCE_LENGTH * MODEL_FEATURES)
    token_groups = tokens.reshape(N_DP, rows, MODEL_FEATURES)
    cotangent_groups = cotangent.reshape(N_DP, rows, MODEL_FEATURES)

    def group(carry, pair):
        block_x, block_dy = pair
        input_float = block_x.astype(jnp.float32)
        inverse_norm = lax.rsqrt(lax.optimization_barrier(jnp.mean(input_float * input_float, axis=1, keepdims=True)) + 1e-05)
        standardized_input = input_float * inverse_norm
        normed_input = (standardized_input * gain).astype(jnp.bfloat16)
        gate = jnp.dot(normed_input, gate_weight, preferred_element_type=jnp.float32)
        up = jnp.dot(normed_input, up_weight, preferred_element_type=jnp.float32)
        sigma = jax.nn.sigmoid(gate)
        swish = gate * sigma
        hidden = (swish * up).astype(jnp.bfloat16)
        back = jnp.dot(block_dy, down_weight.T, preferred_element_type=jnp.float32)
        d_gate = (back * up * sigma * (1.0 + gate * (1.0 - sigma))).astype(jnp.bfloat16)
        d_up = (back * swish).astype(jnp.bfloat16)
        normed_cotangent = jnp.dot(d_gate, gate_weight.T, preferred_element_type=jnp.float32) + jnp.dot(d_up, up_weight.T, preferred_element_type=jnp.float32)
        gain_factor = lax.optimization_barrier(jnp.sum((standardized_input * normed_cotangent).reshape(LOCAL_SEQUENCES, SEQUENCE_LENGTH, MODEL_FEATURES), axis=1))
        hidden3 = hidden.astype(jnp.float32).reshape(LOCAL_SEQUENCES, SEQUENCE_LENGTH, FF)
        dy3 = block_dy.astype(jnp.float32).reshape(LOCAL_SEQUENCES, SEQUENCE_LENGTH, MODEL_FEATURES)
        gram_hidden = jnp.einsum('sif,sjf->sij', hidden3, hidden3)
        gram_dy = jnp.einsum('sid,sjd->sij', dy3, dy3)
        down_sq = lax.optimization_barrier(jnp.sum(gram_hidden * gram_dy, axis=(1, 2)))
        gain_sq = lax.optimization_barrier(jnp.sum(gain_factor * gain_factor, axis=1))
        down_scale = jnp.minimum(1.0, down_bound / (jnp.sqrt(down_sq) + 1e-06)) / SEQS
        gain_scale = jnp.minimum(1.0, gain_bound / (jnp.sqrt(gain_sq) + 1e-06)) / SEQS
        weighted = (jnp.repeat(down_scale, SEQUENCE_LENGTH)[:, None] * block_dy.astype(jnp.float32)).astype(jnp.bfloat16)
        term = jnp.dot(hidden.T, weighted, preferred_element_type=jnp.float32)
        term = lax.optimization_barrier(term.astype(jnp.bfloat16)).astype(jnp.float32)
        gain_part = lax.optimization_barrier(jnp.sum(gain_scale[:, None] * gain_factor, axis=0))
        return ((carry[0] + term, carry[1] + gain_part), None)
    start = (jnp.zeros((FF, MODEL_FEATURES), jnp.float32), jnp.zeros((MODEL_FEATURES,), jnp.float32))
    totals, unused = lax.scan(group, start, (token_groups, cotangent_groups))
    return (totals[0], totals[1])
```

```python
import math

import jax
import jax.numpy as jnp
from jax import lax
from jax.experimental import pallas as pl
from jax.experimental.pallas import tpu as pltpu
from jax.sharding import PartitionSpec as P

MODEL_FEATURES = 4096
FF = 14336
SEQUENCE_LENGTH = 64
NY = 8
NZ = 8
NX = 4


def shift_y(k):
    return [(z * NY + y, z * NY + (y + k) % NY) for z in range(NZ) for y in range(NY)]


def shift_z(k):
    return [(z * NY + y, (z + k) % NZ * NY + y) for z in range(NZ) for y in range(NY)]


def shift_x(k):
    return [(x * 2 + c, (x + k) % NX * 2 + c) for x in range(NX) for c in range(2)]


SWAP = [(x * 2 + c, x * 2 + 1 - c) for x in range(NX) for c in range(2)]


def ring8(block, axis, shift):
    up, down = [block], [block]
    for _ in range(3):
        up.append(lax.ppermute(up[-1], axis, shift(1)))
        down.append(lax.ppermute(down[-1], axis, shift(-1)))
    half = block.shape[0] // 2
    far = jnp.concatenate(
        [
            lax.ppermute(up[3][:half], axis, shift(1)),
            lax.ppermute(down[3][half:], axis, shift(-1)),
        ],
        axis=0,
    )
    return [block, up[1], up[2], up[3], far, down[3], down[2], down[1]]


def place_kernel(outer_is_y, *refs):
    pieces, out, sem = refs[:8], refs[8], refs[9]
    t = lax.axis_index("tensor")
    z, y = t // NY, lax.rem(t, NY)
    for j in range(8):
        for i in range(8):
            if outer_is_y:
                dst = out.at[lax.rem(z - i + 8, 8), lax.rem(y - j + 8, 8)]
            else:
                dst = out.at[lax.rem(z - j + 8, 8), lax.rem(y - i + 8, 8)]
            pltpu.make_async_copy(pieces[j].at[i], dst, sem).start()
    pltpu.make_async_copy(out, out, sem).wait()


def place(pieces, outer_is_y):
    rows, cols = pieces[0].shape[1:]

    def run(*refs):
        place_kernel(outer_is_y, *refs)

    return pl.pallas_call(
        run,
        out_shape=jax.ShapeDtypeStruct((8, 8, rows, cols), pieces[0].dtype),
        in_specs=[pl.BlockSpec(memory_space=pl.ANY)] * 8,
        out_specs=pl.BlockSpec(memory_space=pl.ANY),
        scratch_shapes=[pltpu.SemaphoreType.DMA],
        cost_estimate=pl.CostEstimate(flops=0, bytes_accessed=128 * rows * cols * 2, transcendentals=0),
    )(*pieces)


def gather_features(block, tokens_first):
    rows, cols = block.shape
    first, second = (shift_y, shift_z) if tokens_first else (shift_z, shift_y)
    inner = jnp.stack(ring8(block, "tensor", first))
    pieces = ring8(inner, "tensor", second)
    return place(pieces, not tokens_first).reshape(64 * rows, cols)


def place_columns_kernel(mine, other, out, sem):
    d = lax.axis_index("dp")
    x, c = d // 2, lax.rem(d, 2)
    width = mine.shape[2]
    for j in range(NX):
        src_x = lax.rem(x - j + NX, NX)
        for ref, core in ((mine, c), (other, 1 - c)):
            start = pl.multiple_of((src_x * 2 + core) * width, width)
            pltpu.make_async_copy(ref.at[j], out.at[:, pl.ds(start, width)], sem).start()
    pltpu.make_async_copy(out, out, sem).wait()


def gather_columns(block):
    rows, width = block.shape
    right = lax.ppermute(block, "dp", shift_x(1))
    left = lax.ppermute(block, "dp", shift_x(-1))
    half = rows // 2
    far = jnp.concatenate(
        [
            lax.ppermute(right[:half], "dp", shift_x(1)),
            lax.ppermute(left[half:], "dp", shift_x(-1)),
        ],
        axis=0,
    )
    mine = jnp.stack([block, right, far, left])
    other = lax.ppermute(mine, "dp", SWAP)
    return pl.pallas_call(
        place_columns_kernel,
        out_shape=jax.ShapeDtypeStruct((rows, 8 * width), block.dtype),
        in_specs=[pl.BlockSpec(memory_space=pl.ANY)] * 2,
        out_specs=pl.BlockSpec(memory_space=pl.ANY),
        scratch_shapes=[pltpu.SemaphoreType.DMA],
        cost_estimate=pl.CostEstimate(flops=0, bytes_accessed=32 * rows * width, transcendentals=0),
    )(mine, other)


def body(tokens, gain, cotangent, gate_weight, up_weight, down_weight):
    whole_x = gather_features(tokens.T, True).T
    whole_dy = gather_features(cotangent.T, False).T
    seq_count = whole_x.shape[0] // SEQUENCE_LENGTH
    width = whole_x.shape[1]
    dp_count = lax.axis_size("dp")
    total_seqs = seq_count * dp_count
    input_float = whole_x.astype(jnp.float32)
    inverse_norm = lax.rsqrt(jnp.mean(input_float * input_float, axis=1, keepdims=True) + 1e-05)
    normed_input = (input_float * inverse_norm * gain).astype(jnp.bfloat16)
    gate_full, up_full = (
        lax.all_gather(gate_weight, "dp", axis=0, tiled=True),
        lax.all_gather(up_weight, "dp", axis=0, tiled=True),
    )
    down_full = gather_columns(down_weight)
    gate = jnp.dot(normed_input, gate_full, preferred_element_type=jnp.float32)
    up = jnp.dot(normed_input, up_full, preferred_element_type=jnp.float32)
    contract = (((1,), (1,)), ((), ()))
    back = lax.dot_general(whole_dy, down_full, contract, preferred_element_type=jnp.float32)
    sigma = jax.nn.sigmoid(gate)
    swish = gate * sigma
    hidden = (swish * up).astype(jnp.bfloat16)
    hidden3 = hidden.reshape(seq_count, SEQUENCE_LENGTH, hidden.shape[1])
    cotangent3 = whole_dy.reshape(seq_count, SEQUENCE_LENGTH, width)
    down_part = jnp.einsum("sif,sjf->sij", hidden3, hidden3, preferred_element_type=jnp.float32)
    dy_gram = jnp.einsum("sid,sjd->sij", cotangent3, cotangent3, preferred_element_type=jnp.float32)
    down_sq = lax.psum(jnp.sum(down_part * dy_gram, axis=(1, 2)), "tensor")
    d_gate = (back * up * sigma * (1.0 + gate * (1.0 - sigma))).astype(jnp.bfloat16)
    d_up = (back * swish).astype(jnp.bfloat16)
    normed_cotangent = lax.dot_general(
        d_gate, gate_full, contract, preferred_element_type=jnp.float32
    ) + lax.dot_general(d_up, up_full, contract, preferred_element_type=jnp.float32)
    gain_factor = jnp.sum(
        (input_float * inverse_norm * normed_cotangent).reshape(seq_count, SEQUENCE_LENGTH, width),
        axis=1,
    )
    gain_mine = lax.psum_scatter(gain_factor, "tensor", scatter_dimension=1, tiled=True)
    gain_mine, down_sq = lax.optimization_barrier((gain_mine, down_sq))
    gain_sq = lax.psum(jnp.sum(gain_mine * gain_mine, axis=1), "tensor")
    down_bound = 0.6 * math.sqrt(SEQUENCE_LENGTH * FF * MODEL_FEATURES)
    gain_bound = 0.5 * math.sqrt(SEQUENCE_LENGTH * MODEL_FEATURES)
    down_scale = jnp.minimum(1.0, down_bound / (jnp.sqrt(down_sq) + 1e-06)) / total_seqs
    gain_scale = jnp.minimum(1.0, gain_bound / (jnp.sqrt(gain_sq) + 1e-06)) / total_seqs
    gain_local = jnp.sum(gain_scale[:, None] * gain_mine, axis=0)
    grad_gain = lax.psum(gain_local, "dp")
    weighted = (
        jnp.repeat(down_scale, SEQUENCE_LENGTH)[:, None] * whole_dy.astype(jnp.float32)
    ).astype(jnp.bfloat16)
    terms = jnp.einsum(
        "tu,tdf->duf", hidden, weighted.reshape(-1, dp_count, width // dp_count),
        preferred_element_type=jnp.float32,
    ).astype(jnp.bfloat16)
    shared = lax.all_to_all(terms, "dp", split_axis=0, concat_axis=0, tiled=True)
    return (jnp.sum(shared.astype(jnp.float32), axis=0), grad_gain)


def solution(mesh):
    in_specs = (
        P("dp", "tensor"),
        P(),
        P("dp", "tensor"),
        P("dp", "tensor"),
        P("dp", "tensor"),
        P("tensor", "dp"),
    )
    out_specs = (P("tensor", "dp"), P("tensor"))
    return jax.shard_map(body, mesh=mesh, in_specs=in_specs, out_specs=out_specs, check_vma=False)
```

```python
import math

import jax
import jax.numpy as jnp
from jax import lax
from jax.experimental import pallas as pl
from jax.experimental.pallas import tpu as pltpu
from jax.sharding import Mesh
from jax.sharding import PartitionSpec as P

FEATURES = 4096
FF = 14336
SEQ = 64
SEQS = 64
NX, NC, NZ, NY = 4, 2, 8, 8
LOCAL = 8
TOK = LOCAL * SEQ
UNITS = FF // (NZ * NY)
SHARE = FEATURES // (NX * NC)
COLS = FEATURES // (NZ * NY)
F32 = jnp.float32
BF16 = jnp.bfloat16

SMEM = pl.BlockSpec(memory_space=pltpu.SMEM)
VMEM = pl.BlockSpec(memory_space=pltpu.VMEM)


def params(mib):
    return pltpu.CompilerParams(vmem_limit_bytes=mib * 1024 * 1024)


def cost(macs, nbytes):
    return pl.CostEstimate(flops=2 * macs, bytes_accessed=nbytes, transcendentals=0)


def each_share(idx, body):
    core = idx[1]

    def step(i, carry):
        body(i, 0, 2 * i + core)
        body(i, 1, 2 * i + 1 - core)
        return carry

    lax.fori_loop(0, NX, step, 0)


def hidden_kernel(idx, *refs):
    pieces, (mine, other, gain, xs, gate, up, hidden, inverse, acc) = refs[:NZ], refs[NZ:]
    z = idx[0]
    total = jnp.zeros((8, TOK), F32)
    for j in range(NZ):
        slot = lax.rem(z - j + NZ, NZ)
        for i in range(NY):
            block = pieces[j][i]
            xs[slot, pl.ds(i * COLS, COLS), :] = block
            wide = block.astype(F32)
            total += jnp.sum((wide * wide).reshape(COLS // 8, 8, TOK), axis=0)
    mean = jnp.sum(total, axis=0, keepdims=True) * (1.0 / FEATURES)
    inverse[...] = lax.rsqrt(mean + 1e-05)
    acc[...] = jnp.zeros_like(acc)

    def share(i, which, d):
        ref = other if which else mine
        scaled = ref[i].reshape(2 * UNITS, SHARE).astype(F32) * gain[pl.ds(d, 1), :]
        acc[...] += jnp.dot(scaled.astype(BF16), xs[d], preferred_element_type=F32)

    each_share(idx, share)

    def rows(i, carry):
        r = pl.multiple_of(i * 32, 32)
        inv = inverse[...]
        g = acc[pl.ds(r, 32), :] * inv
        u = acc[pl.ds(pl.multiple_of(UNITS + r, 32), 32), :] * inv
        gate[pl.ds(r, 32), :] = g
        up[pl.ds(r, 32), :] = u
        hidden[pl.ds(r, 32), :] = (g * jax.nn.sigmoid(g) * u).astype(BF16)
        return carry

    lax.fori_loop(0, UNITS // 32, rows, 0)


def hidden_call(idx, pieces, mine, other, gain):
    return pl.pallas_call(
        hidden_kernel,
        out_shape=(
            jax.ShapeDtypeStruct((NZ, SHARE, TOK), BF16),
            jax.ShapeDtypeStruct((UNITS, TOK), F32),
            jax.ShapeDtypeStruct((UNITS, TOK), F32),
            jax.ShapeDtypeStruct((UNITS, TOK), BF16),
            jax.ShapeDtypeStruct((1, TOK), F32),
        ),
        in_specs=[SMEM] + [VMEM] * (NZ + 3),
        out_specs=(VMEM,) * 5,
        scratch_shapes=[pltpu.VMEM((2 * UNITS, TOK), F32)],
        compiler_params=params(40),
        cost_estimate=cost(2 * UNITS * TOK * FEATURES, 14 << 20),
        name="hidden",
    )(idx, *pieces, mine, other, gain)


TN = (((0,), (0,)), ((), ()))
NT = (((1,), (1,)), ((), ()))


def gram_kernel(dy, hidden, out):
    half = TOK // 2
    for h in range(2):
        lanes = slice(h * half, (h + 1) * half)
        mine = hidden[:, lanes]
        own = lax.dot_general(mine, mine, TN, preferred_element_type=F32)

        def step(z, acc):
            block = dy[:, z, :, lanes].reshape(SHARE, half)
            return acc + lax.dot_general(block, block, TN, preferred_element_type=F32)

        pairs = own * lax.fori_loop(0, NZ, step, jnp.zeros((half, half), F32))
        for s in range(half // SEQ):
            part = pairs[s * SEQ : (s + 1) * SEQ, s * SEQ : (s + 1) * SEQ]
            value = jnp.sum(jnp.sum(part, axis=0, keepdims=True), axis=1, keepdims=True)
            i = h * (half // SEQ) + s
            out[:, i : i + 1, :] = jnp.broadcast_to(value.reshape(1, 1, 1), (NY, 1, 128))


def gram_call(dy, hidden):
    return pl.pallas_call(
        gram_kernel,
        out_shape=jax.ShapeDtypeStruct((NY, LOCAL, 128), F32),
        in_specs=[VMEM] * 2,
        out_specs=VMEM,
        compiler_params=params(24),
        cost_estimate=cost(TOK * TOK * (FEATURES + UNITS), 5 << 20),
        name="gram",
    )(dy, hidden)


def back_kernel(idx, dy, mine, other, gate, up, grads, acc):
    acc[...] = jnp.zeros_like(acc)

    def share(i, which, d):
        ref = other if which else mine
        block = dy[:, d, :, :].reshape(SHARE, TOK)
        acc[...] += jnp.dot(ref[i], block, preferred_element_type=F32)

    each_share(idx, share)

    def rows(i, carry):
        r = pl.multiple_of(i * 32, 32)
        b, g, u = acc[pl.ds(r, 32), :], gate[pl.ds(r, 32), :], up[pl.ds(r, 32), :]
        sigma = jax.nn.sigmoid(g)
        grads[pl.ds(r, 32), :] = (b * u * sigma * (1.0 + g * (1.0 - sigma))).astype(BF16)
        grads[pl.ds(pl.multiple_of(UNITS + r, 32), 32), :] = (b * g * sigma).astype(BF16)
        return carry

    lax.fori_loop(0, UNITS // 32, rows, 0)


def back_call(idx, dy, mine, other, gate, up):
    return pl.pallas_call(
        back_kernel,
        out_shape=jax.ShapeDtypeStruct((2 * UNITS, TOK), BF16),
        in_specs=[SMEM] + [VMEM] * 5,
        out_specs=VMEM,
        scratch_shapes=[pltpu.VMEM((UNITS, TOK), F32)],
        compiler_params=params(28),
        cost_estimate=cost(UNITS * TOK * FEATURES, 7 << 20),
        name="back",
    )(idx, dy, mine, other, gate, up)


def gain_kernel(idx, grads, inverse, xs, mine, other, out):
    token = lax.broadcasted_iota(jnp.int32, (TOK, 128), 0)
    column = lax.broadcasted_iota(jnp.int32, (TOK, 128), 1)
    select = jnp.where(token // SEQ == column, 1.0, 0.0).astype(BF16)
    core = idx[1]
    wide = SHARE // 2

    def term(weight, d, h):
        f = slice(h * wide, (h + 1) * wide)
        normed = lax.dot_general(weight[:, f], grads[...], TN, preferred_element_type=F32)
        product = xs[d, f, :].astype(F32) * inverse[...] * normed
        high = product.astype(BF16)
        low = (product - high.astype(F32)).astype(BF16)
        total = jnp.dot(high, select, preferred_element_type=F32)
        total += jnp.dot(low, select, preferred_element_type=F32)
        return total.T[:LOCAL]

    def step(i, carry):
        for h in range(2):
            a = term(mine[i].reshape(2 * UNITS, SHARE), 2 * i + core, h)
            b = term(other[i].reshape(2 * UNITS, SHARE), 2 * i + 1 - core, h)
            even, odd = jnp.where(core == 0, a, b), jnp.where(core == 0, b, a)
            for y in range(wide // COLS):
                lanes = slice(y * COLS, (y + 1) * COLS)
                rows = pl.ds(pl.multiple_of(i * LOCAL, LOCAL), LOCAL)
                out[h * (wide // COLS) + y, rows, :] = jnp.concatenate([even[:, lanes], odd[:, lanes]], axis=1)
        return carry

    lax.fori_loop(0, NX, step, 0)


def gain_call(idx, grads, inverse, xs, mine, other):
    return pl.pallas_call(
        gain_kernel,
        out_shape=jax.ShapeDtypeStruct((NY, NX * LOCAL, 128), F32),
        in_specs=[SMEM] + [VMEM] * 5,
        out_specs=VMEM,
        compiler_params=params(40),
        cost_estimate=cost(3 * UNITS * TOK * FEATURES, 9 << 20),
        name="gain_term",
    )(idx, grads, inverse, xs, mine, other)


def add_kernel(part, out):
    out[...] = jnp.broadcast_to(jnp.sum(part[...], axis=0, keepdims=True), out.shape)


def add_and_repeat(part):
    return pl.pallas_call(add_kernel, out_shape=jax.ShapeDtypeStruct(part.shape, F32), name="add_parts")(part)


def gain_sq_kernel(part, total, square):
    whole = jnp.sum(part[...], axis=0)
    total[...] = whole
    rows = jnp.sum((whole * whole).reshape(NX, LOCAL, 128), axis=0)
    value = jnp.sum(rows, axis=1, keepdims=True)
    square[...] = jnp.broadcast_to(value[None], square.shape)


def gain_scale_kernel(idx, part, total, out):
    square = jnp.sum(part[...], axis=0)
    bound = 0.5 * math.sqrt(SEQ * FEATURES)
    scale = jnp.minimum(1.0, bound / (jnp.sqrt(square) + 1e-06)) / SEQS
    rows = total[pl.ds(pl.multiple_of(idx[0] // 2 * LOCAL, LOCAL), LOCAL), :]
    value = jnp.sum(scale * rows, axis=0, keepdims=True)
    out[...] = jnp.broadcast_to(value[None], out.shape)


def grad_kernel(down_sq, hidden, dy, out):
    bound = 0.6 * math.sqrt(SEQ * FF * FEATURES)
    total = jnp.sum(down_sq[...], axis=0)
    scale = jnp.minimum(1.0, bound / (jnp.sqrt(total) + 1e-06)) / SEQS
    first = lax.broadcasted_iota(jnp.int32, (1, 128), 1) < SEQ
    row = jnp.concatenate(
        [jnp.where(first, scale[2 * k : 2 * k + 1], scale[2 * k + 1 : 2 * k + 2]) for k in range(LOCAL // 2)],
        axis=1,
    )
    scaled = (hidden[...].astype(F32) * row).astype(BF16)

    def step(d, carry):
        block = dy[:, d, :, :].reshape(SHARE, TOK)
        out[d] = lax.dot_general(scaled, block, NT, preferred_element_type=F32).astype(BF16)
        return carry

    lax.fori_loop(0, NX * NC, step, 0)


def grad_call(down_sq, hidden, dy):
    return pl.pallas_call(
        grad_kernel,
        out_shape=jax.ShapeDtypeStruct((NX * NC, UNITS, SHARE), BF16),
        in_specs=[VMEM] * 3,
        out_specs=VMEM,
        compiler_params=params(24),
        cost_estimate=cost(UNITS * TOK * FEATURES, 6 << 20),
        name="grad_down",
    )(down_sq, hidden, dy)


def spread(block, axis, count):
    return lax.all_to_all(
        jnp.broadcast_to(block[None], (count,) + block.shape), axis, split_axis=0, concat_axis=0, tiled=True
    )


def exchange(blocks, axis):
    return lax.all_to_all(blocks, axis, split_axis=0, concat_axis=0, tiled=True)


def ring(block, axis, size):
    shift = lambda k: [(i, (i + k) % size) for i in range(size)]
    up, down = [block], [block]
    for step in range(size // 2):
        up.append(lax.ppermute(up[-1], axis, shift(1)))
        if step < size // 2 - 1:
            down.append(lax.ppermute(down[-1], axis, shift(-1)))
    return up + down[:0:-1]


def body(tokens, gain, cotangent, gate_weight, up_weight, down_weight):
    idx = jnp.stack([lax.axis_index("z"), lax.axis_index("core")]).astype(jnp.int32)
    x_part = spread(tokens.T, "y", NY)
    both = jnp.stack([gate_weight.T, up_weight.T])
    mine = spread(both, "x", NX)
    dy_part = spread(cotangent.T, "z", NZ)
    dmine = spread(down_weight, "x", NX)
    swap = [(0, 1), (1, 0)]
    pieces = ring(x_part, "z", NZ)
    dy = lax.all_gather(dy_part, "y", axis=0)
    other = lax.ppermute(mine, "core", swap)
    dother = lax.ppermute(dmine, "core", swap)

    xs, gate, up, hidden, inverse = hidden_call(idx, pieces, mine, other, gain.reshape(NX * NC, SHARE))
    gram = gram_call(dy, hidden)
    part = exchange(gram, "y")
    dy_back, gram = lax.optimization_barrier((dy, gram))
    grads = back_call(idx, dy_back, dmine, dother, gate, up)
    part, grads = lax.optimization_barrier((part, grads))
    down_sq = exchange(add_and_repeat(part), "z")
    gain_part = gain_call(idx, grads, inverse, xs, mine, other)
    down_sq, gain_part = lax.optimization_barrier((down_sq, gain_part))
    terms = grad_call(down_sq, hidden, dy)
    grad = exchange(terms, ("x", "core"))
    gain_part, terms = lax.optimization_barrier((gain_part, terms))

    gain_part = exchange(add_and_repeat(exchange(gain_part, "y")), "z")
    gain_y, sq_part = pl.pallas_call(
        gain_sq_kernel,
        out_shape=(
            jax.ShapeDtypeStruct((NX * LOCAL, 128), F32),
            jax.ShapeDtypeStruct((NY, LOCAL, 128), F32),
        ),
        name="gain_sq",
    )(gain_part)
    gain_local = pl.pallas_call(
        gain_scale_kernel,
        out_shape=jax.ShapeDtypeStruct((NX * NC, 8, 128), F32),
        in_specs=[SMEM, VMEM, VMEM],
        name="gain_scale",
    )(idx, exchange(sq_part, "y"), gain_y)
    gain_all = jnp.sum(exchange(gain_local, ("x", "core"))[:, 0], axis=0)
    grad_gain = jnp.where(idx[0] % 2 == 0, gain_all[:COLS], gain_all[COLS:])
    grad_down = jnp.sum(grad.astype(F32), axis=0)
    return (grad_down, grad_gain)


def solution(mesh):
    split = Mesh(mesh.devices.reshape(NX, NC, NZ, NY), ("x", "core", "z", "y"))
    dp, tensor = ("x", "core"), ("z", "y")
    in_specs = (P(dp, tensor), P(), P(dp, tensor), P(dp, tensor), P(dp, tensor), P(tensor, dp))
    out_specs = (P(tensor, dp), P(tensor))
    return jax.shard_map(body, mesh=split, in_specs=in_specs, out_specs=out_specs, check_vma=False)
```

```python
import math

import jax
import jax.numpy as jnp
from jax import lax
from jax.experimental import pallas as pl
from jax.experimental.pallas import tpu as pltpu
from jax.sharding import Mesh
from jax.sharding import PartitionSpec as P

FEATURES = 4096
FF = 14336
SEQ = 64
SEQS = 64
NX, NC, NZ, NY = 4, 2, 8, 8
LOCAL = 8
TOK = LOCAL * SEQ
UNITS = FF // (NZ * NY)
SHARE = FEATURES // (NX * NC)
COLS = FEATURES // (NZ * NY)
F32 = jnp.float32
BF16 = jnp.bfloat16

SMEM = pl.BlockSpec(memory_space=pltpu.SMEM)
VMEM = pl.BlockSpec(memory_space=pltpu.VMEM)


def params(mib):
    return pltpu.CompilerParams(vmem_limit_bytes=mib * 1024 * 1024)


def cost(macs, nbytes):
    return pl.CostEstimate(flops=2 * macs, bytes_accessed=nbytes, transcendentals=0)


def each_share(idx, body):
    core = idx[1]

    def step(i, carry):
        body(i, 0, 2 * i + core)
        body(i, 1, 2 * i + 1 - core)
        return carry

    lax.fori_loop(0, NX, step, 0)


TN = (((0,), (0,)), ((), ()))
NT = (((1,), (1,)), ((), ()))
HALF = TOK // 2


def cotangent_kernel(idx, *refs):
    pieces, (dy, gram) = refs[:NY], refs[NY:]
    y = idx[2]
    for j in range(NY):
        slot = lax.rem(y - j + NY, NY)
        for i in range(NZ):
            dy[i, pl.ds(pl.multiple_of(slot * COLS, COLS), COLS), :] = pieces[j][i]
    for h in range(2):

        def step(z, acc):
            block = dy[z, :, h * HALF : (h + 1) * HALF]
            return acc + lax.dot_general(block, block, TN, preferred_element_type=F32)

        gram[h] = lax.fori_loop(0, NZ, step, jnp.zeros((HALF, HALF), F32))


def cotangent_call(idx, pieces):
    return pl.pallas_call(
        cotangent_kernel,
        out_shape=(
            jax.ShapeDtypeStruct((NZ, SHARE, TOK), BF16),
            jax.ShapeDtypeStruct((2, HALF, HALF), F32),
        ),
        in_specs=[SMEM] + [VMEM] * NY,
        out_specs=(VMEM,) * 2,
        compiler_params=params(16),
        cost_estimate=cost(TOK * HALF * FEATURES, 9 << 20),
        name="cotangent_gram",
    )(idx, *pieces)


def hidden_kernel(idx, *refs):
    pieces, (wg, wu, gain, dy_gram, xs, gate, up, hidden, inverse, down_sq, acc) = refs[:NZ], refs[NZ:]
    z = idx[0]
    total = jnp.zeros((8, TOK), F32)
    for j in range(NZ):
        slot = lax.rem(z - j + NZ, NZ)
        for i in range(NY):
            block = pieces[j][i]
            xs[slot, pl.ds(i * COLS, COLS), :] = block
            wide = block.astype(F32)
            total += jnp.sum((wide * wide).reshape(COLS // 8, 8, TOK), axis=0)
    mean = jnp.sum(total, axis=0, keepdims=True) * (1.0 / FEATURES)
    inverse[...] = lax.rsqrt(mean + 1e-05)
    acc[...] = jnp.zeros_like(acc)

    def share(d, carry):
        row = gain[pl.ds(d, 1), :]
        for k, ref in enumerate((wg, wu)):
            scaled = (ref[d].astype(F32) * row).astype(BF16)
            acc[k] += jnp.dot(scaled, xs[d], preferred_element_type=F32)
        return carry

    lax.fori_loop(0, NX * NC, share, 0)

    def rows(i, carry):
        r = pl.ds(pl.multiple_of(i * 32, 32), 32)
        inv = inverse[...]
        g = acc[0, r, :] * inv
        u = acc[1, r, :] * inv
        gate[r, :] = g
        up[r, :] = u
        hidden[r, :] = (g * jax.nn.sigmoid(g) * u).astype(BF16)
        return carry

    lax.fori_loop(0, UNITS // 32, rows, 0)
    for h in range(2):
        own = hidden[:, h * HALF : (h + 1) * HALF]
        pairs = lax.dot_general(own, own, TN, preferred_element_type=F32) * dy_gram[h]
        for s in range(HALF // SEQ):
            part = pairs[s * SEQ : (s + 1) * SEQ, s * SEQ : (s + 1) * SEQ]
            value = jnp.sum(jnp.sum(part, axis=0, keepdims=True), axis=1, keepdims=True)
            i = h * (HALF // SEQ) + s
            down_sq[:, i : i + 1, :] = jnp.broadcast_to(value.reshape(1, 1, 1), (NY, 1, 128))


def hidden_call(idx, pieces, wg, wu, gain, dy_gram):
    return pl.pallas_call(
        hidden_kernel,
        out_shape=(
            jax.ShapeDtypeStruct((NZ, SHARE, TOK), BF16),
            jax.ShapeDtypeStruct((UNITS, TOK), F32),
            jax.ShapeDtypeStruct((UNITS, TOK), F32),
            jax.ShapeDtypeStruct((UNITS, TOK), BF16),
            jax.ShapeDtypeStruct((1, TOK), F32),
            jax.ShapeDtypeStruct((NY, LOCAL, 128), F32),
        ),
        in_specs=[SMEM] + [VMEM] * (NZ + 4),
        out_specs=(VMEM,) * 6,
        scratch_shapes=[pltpu.VMEM((2, UNITS, TOK), F32)],
        compiler_params=params(24),
        cost_estimate=cost(2 * UNITS * TOK * FEATURES, 14 << 20),
        name="hidden",
    )(idx, *pieces, wg, wu, gain, dy_gram)


def back_kernel(idx, dy, mine, other, gate, up, grads, acc):
    acc[...] = jnp.zeros_like(acc)

    def share(i, which, d):
        ref = other if which else mine
        acc[...] += jnp.dot(ref[i], dy[d], preferred_element_type=F32)

    each_share(idx, share)

    def rows(i, carry):
        r = pl.multiple_of(i * 32, 32)
        b, g, u = acc[pl.ds(r, 32), :], gate[pl.ds(r, 32), :], up[pl.ds(r, 32), :]
        sigma = jax.nn.sigmoid(g)
        grads[pl.ds(r, 32), :] = (b * u * sigma * (1.0 + g * (1.0 - sigma))).astype(BF16)
        grads[pl.ds(pl.multiple_of(UNITS + r, 32), 32), :] = (b * g * sigma).astype(BF16)
        return carry

    lax.fori_loop(0, UNITS // 32, rows, 0)


def back_call(idx, dy, mine, other, gate, up):
    return pl.pallas_call(
        back_kernel,
        out_shape=jax.ShapeDtypeStruct((2 * UNITS, TOK), BF16),
        in_specs=[SMEM] + [VMEM] * 5,
        out_specs=VMEM,
        scratch_shapes=[pltpu.VMEM((UNITS, TOK), F32)],
        compiler_params=params(16),
        cost_estimate=cost(UNITS * TOK * FEATURES, 7 << 20),
        name="back",
    )(idx, dy, mine, other, gate, up)


def gain_kernel(grads, inverse, xs, wg, wu, out):
    token = lax.broadcasted_iota(jnp.int32, (TOK, 128), 0)
    column = lax.broadcasted_iota(jnp.int32, (TOK, 128), 1)
    select = jnp.where(token // SEQ == column, 1.0, 0.0).astype(BF16)
    wide = SHARE // 2

    def term(d, h):
        f = slice(h * wide, (h + 1) * wide)
        normed = lax.dot_general(wg[d, :, f], grads[:UNITS], TN, preferred_element_type=F32)
        normed += lax.dot_general(wu[d, :, f], grads[UNITS:], TN, preferred_element_type=F32)
        product = xs[d, f, :].astype(F32) * inverse[...] * normed
        high = product.astype(BF16)
        low = (product - high.astype(F32)).astype(BF16)
        total = jnp.dot(high, select, preferred_element_type=F32)
        total += jnp.dot(low, select, preferred_element_type=F32)
        return total.T[:LOCAL]

    def step(i, carry):
        for h in range(2):
            even, odd = term(2 * i, h), term(2 * i + 1, h)
            for y in range(wide // COLS):
                lanes = slice(y * COLS, (y + 1) * COLS)
                rows = pl.ds(pl.multiple_of(i * LOCAL, LOCAL), LOCAL)
                out[h * (wide // COLS) + y, rows, :] = jnp.concatenate([even[:, lanes], odd[:, lanes]], axis=1)
        return carry

    lax.fori_loop(0, NX, step, 0)


def gain_call(grads, inverse, xs, wg, wu):
    return pl.pallas_call(
        gain_kernel,
        out_shape=jax.ShapeDtypeStruct((NY, NX * LOCAL, 128), F32),
        in_specs=[VMEM] * 5,
        out_specs=VMEM,
        compiler_params=params(20),
        cost_estimate=cost(3 * UNITS * TOK * FEATURES, 9 << 20),
        name="gain_term",
    )(grads, inverse, xs, wg, wu)


def add_kernel(part, out):
    out[...] = jnp.broadcast_to(jnp.sum(part[...], axis=0, keepdims=True), out.shape)


def add_and_repeat(part):
    return pl.pallas_call(add_kernel, out_shape=jax.ShapeDtypeStruct(part.shape, F32), name="add_parts")(part)


def gain_sq_kernel(part, total, square):
    whole = jnp.sum(part[...], axis=0)
    total[...] = whole
    rows = jnp.sum((whole * whole).reshape(NX, LOCAL, 128), axis=0)
    value = jnp.sum(rows, axis=1, keepdims=True)
    square[...] = jnp.broadcast_to(value[None], square.shape)


def gain_scale_kernel(idx, part, total, out):
    square = jnp.sum(part[...], axis=0)
    bound = 0.5 * math.sqrt(SEQ * FEATURES)
    scale = jnp.minimum(1.0, bound / (jnp.sqrt(square) + 1e-06)) / SEQS
    rows = total[pl.ds(pl.multiple_of(idx[0] // 2 * LOCAL, LOCAL), LOCAL), :]
    value = jnp.sum(scale * rows, axis=0, keepdims=True)
    out[...] = jnp.broadcast_to(value[None], out.shape)


def grad_kernel(down_sq, hidden, dy, out):
    bound = 0.6 * math.sqrt(SEQ * FF * FEATURES)
    total = jnp.sum(down_sq[...], axis=0)
    scale = jnp.minimum(1.0, bound / (jnp.sqrt(total) + 1e-06)) / SEQS
    first = lax.broadcasted_iota(jnp.int32, (1, 128), 1) < SEQ
    row = jnp.concatenate(
        [jnp.where(first, scale[2 * k : 2 * k + 1], scale[2 * k + 1 : 2 * k + 2]) for k in range(LOCAL // 2)],
        axis=1,
    )
    scaled = (hidden[...].astype(F32) * row).astype(BF16)

    def step(d, carry):
        out[d] = lax.dot_general(scaled, dy[d], NT, preferred_element_type=F32).astype(BF16)
        return carry

    lax.fori_loop(0, NX * NC, step, 0)


def grad_call(down_sq, hidden, dy):
    return pl.pallas_call(
        grad_kernel,
        out_shape=jax.ShapeDtypeStruct((NX * NC, UNITS, SHARE), BF16),
        in_specs=[VMEM] * 3,
        out_specs=VMEM,
        compiler_params=params(14),
        cost_estimate=cost(UNITS * TOK * FEATURES, 6 << 20),
        name="grad_down",
    )(down_sq, hidden, dy)


def spread(block, axis, count):
    return lax.all_to_all(
        jnp.broadcast_to(block[None], (count,) + block.shape), axis, split_axis=0, concat_axis=0, tiled=True
    )


def exchange(blocks, axis):
    return lax.all_to_all(blocks, axis, split_axis=0, concat_axis=0, tiled=True)


def ring(block, axis, size):
    shift = lambda k: [(i, (i + k) % size) for i in range(size)]
    up, down = [block], [block]
    for step in range(size // 2):
        up.append(lax.ppermute(up[-1], axis, shift(1)))
        if step < size // 2 - 1:
            down.append(lax.ppermute(down[-1], axis, shift(-1)))
    return up + down[:0:-1]


def body(tokens, gain, cotangent, gate_weight, up_weight, down_weight):
    idx = jnp.stack([lax.axis_index("z"), lax.axis_index("core"), lax.axis_index("y")]).astype(jnp.int32)
    dp = ("x", "core")
    x_part = lax.all_gather(tokens.T, "y", axis=0)
    wg = lax.all_gather(gate_weight.T, dp, axis=0)
    wu = lax.all_gather(up_weight.T, dp, axis=0)
    dy_part = spread(cotangent.T, "z", NZ)
    dmine = spread(down_weight, "x", NX)
    dy_pieces = ring(dy_part, "y", NY)
    pieces = ring(x_part, "z", NZ)
    dother = lax.ppermute(dmine, "core", [(0, 1), (1, 0)])

    dy, dy_gram = cotangent_call(idx, dy_pieces)
    xs, gate, up, hidden, inverse, sq_part = hidden_call(
        idx, pieces, wg, wu, gain.reshape(NX * NC, SHARE), dy_gram
    )
    part = exchange(sq_part, "y")
    dy_back, sq_part = lax.optimization_barrier((dy, sq_part))
    grads = back_call(idx, dy_back, dmine, dother, gate, up)
    part, grads = lax.optimization_barrier((part, grads))
    down_sq = exchange(add_and_repeat(part), "z")
    gain_part = gain_call(grads, inverse, xs, wg, wu)
    down_sq, gain_part = lax.optimization_barrier((down_sq, gain_part))
    terms = grad_call(down_sq, hidden, dy)
    grad_down = lax.psum_scatter(terms, dp, scatter_dimension=0).astype(F32)

    gain_part = exchange(add_and_repeat(exchange(gain_part, "y")), "z")
    gain_y, sq_part = pl.pallas_call(
        gain_sq_kernel,
        out_shape=(
            jax.ShapeDtypeStruct((NX * LOCAL, 128), F32),
            jax.ShapeDtypeStruct((NY, LOCAL, 128), F32),
        ),
        name="gain_sq",
    )(gain_part)
    gain_local = pl.pallas_call(
        gain_scale_kernel,
        out_shape=jax.ShapeDtypeStruct((NX * NC, 8, 128), F32),
        in_specs=[SMEM, VMEM, VMEM],
        name="gain_scale",
    )(idx, exchange(sq_part, "y"), gain_y)
    gain_all = jnp.sum(exchange(gain_local, ("x", "core"))[:, 0], axis=0)
    grad_gain = jnp.where(idx[0] % 2 == 0, gain_all[:COLS], gain_all[COLS:])
    return (grad_down, grad_gain)


def solution(mesh):
    split = Mesh(mesh.devices.reshape(NX, NC, NZ, NY), ("x", "core", "z", "y"))
    dp, tensor = ("x", "core"), ("z", "y")
    in_specs = (P(dp, tensor), P(), P(dp, tensor), P(dp, tensor), P(dp, tensor), P(tensor, dp))
    out_specs = (P(tensor, dp), P(tensor))
    return jax.shard_map(body, mesh=split, in_specs=in_specs, out_specs=out_specs, check_vma=False)
```

```python
import math

import jax
import jax.numpy as jnp
from jax import lax
from jax.experimental import pallas as pl
from jax.experimental.pallas import tpu as pltpu
from jax.sharding import Mesh
from jax.sharding import PartitionSpec as P

FEATURES = 4096
FF = 14336
SEQ = 64
SEQS = 64
NX, NC, NZ, NY = 4, 2, 8, 8
LOCAL = 8
TOK = LOCAL * SEQ
UNITS = FF // (NZ * NY)
SHARE = FEATURES // (NX * NC)
COLS = FEATURES // (NZ * NY)
F32 = jnp.float32
BF16 = jnp.bfloat16

SMEM = pl.BlockSpec(memory_space=pltpu.SMEM)
VMEM = pl.BlockSpec(memory_space=pltpu.VMEM)


def params(mib):
    return pltpu.CompilerParams(vmem_limit_bytes=mib * 1024 * 1024)


def cost(macs, nbytes):
    return pl.CostEstimate(flops=2 * macs, bytes_accessed=nbytes, transcendentals=0)


TN = (((0,), (0,)), ((), ()))
NT = (((1,), (1,)), ((), ()))
HALF = TOK // 2
ANY = pl.BlockSpec(memory_space=pl.ANY)


def whole(shape):
    return pl.BlockSpec(shape, lambda i: (0,) * len(shape))


def lead(shape):
    return pl.BlockSpec(shape, lambda i: (i,) + (0,) * (len(shape) - 1))


def cotangent_kernel(idx, *refs):
    pieces, (dy, gram, held, sems, out_sem) = refs[:NY], refs[NY:]
    y = idx[2]
    for j in range(NY):
        slot = lax.rem(y - j + NY, NY)
        pltpu.make_async_copy(pieces[j], held.at[:, slot], sems.at[j]).start()
    for j in range(NY):
        slot = lax.rem(y - j + NY, NY)
        pltpu.make_async_copy(pieces[j], held.at[:, slot], sems.at[j]).wait()
    keep = pltpu.make_async_copy(held, dy, out_sem)
    keep.start()
    for h in range(2):

        def step(z, acc):
            block = held[z, :, :, h * HALF : (h + 1) * HALF].reshape(SHARE, HALF)
            return acc + lax.dot_general(block, block, TN, preferred_element_type=F32)

        gram[h] = lax.fori_loop(0, NZ, step, jnp.zeros((HALF, HALF), F32))
    keep.wait()


def cotangent_call(idx, pieces):
    return pl.pallas_call(
        cotangent_kernel,
        out_shape=(
            jax.ShapeDtypeStruct((NZ, NY, COLS, TOK), BF16),
            jax.ShapeDtypeStruct((2, HALF, HALF), F32),
        ),
        in_specs=[SMEM] + [ANY] * NY,
        out_specs=(ANY, VMEM),
        scratch_shapes=[
            pltpu.VMEM((NZ, NY, COLS, TOK), BF16),
            pltpu.SemaphoreType.DMA((NY,)),
            pltpu.SemaphoreType.DMA,
        ],
        compiler_params=params(24),
        cost_estimate=cost(TOK * HALF * FEATURES, 9 << 20),
        name="cotangent_gram",
    )(idx, *pieces)


def back_kernel(idx, dy, mine, other, back):
    core = idx[1]

    @pl.when(pl.program_id(0) == 0)
    def _():
        back[...] = jnp.zeros_like(back)

    back[...] += jnp.dot(mine[0], dy[core].reshape(SHARE, TOK), preferred_element_type=F32)
    back[...] += jnp.dot(other[0], dy[1 - core].reshape(SHARE, TOK), preferred_element_type=F32)


def back_call(idx, dy, mine, other):
    return pl.pallas_call(
        back_kernel,
        grid=(NX,),
        out_shape=jax.ShapeDtypeStruct((UNITS, TOK), F32),
        in_specs=[SMEM, lead((2, NY, COLS, TOK)), lead((1, UNITS, SHARE)), lead((1, UNITS, SHARE))],
        out_specs=whole((UNITS, TOK)),
        compiler_params=params(24),
        cost_estimate=cost(UNITS * TOK * FEATURES, 7 << 20),
        name="back",
    )(idx, dy, mine, other)


def hidden_kernel(idx, *refs):
    pieces, (wg, wu, gain, dy_gram, back, xs, hidden, inverse, down_sq, grads) = refs[:NZ], refs[NZ : NZ + 10]
    x, g_held, u_held, acc, sems, out_sems = refs[NZ + 10 :]
    z = idx[0]

    def copies(j, source):
        d = lax.rem(z - j + NZ, NZ)
        return (
            pltpu.make_async_copy(source, x.at[d], sems.at[0, j]),
            pltpu.make_async_copy(wg.at[d], g_held.at[d], sems.at[1, j]),
            pltpu.make_async_copy(wu.at[d], u_held.at[d], sems.at[2, j]),
        )

    for j in range(NZ):
        for copy in copies(j, pieces[j]):
            copy.start()
    acc[...] = jnp.zeros_like(acc)

    def keep(j):
        d = lax.rem(z - j + NZ, NZ)
        return pltpu.make_async_copy(x.at[d], xs.at[d], out_sems.at[j])

    def share(j, total):
        d = lax.rem(z - j + NZ, NZ)
        for copy in copies(j, pieces[0]):
            copy.wait()
        keep(j).start()
        row = gain[pl.ds(d, 1), :]
        block = x[d].reshape(SHARE, TOK)
        for k, ref in enumerate((g_held, u_held)):
            scaled = (ref[d].astype(F32) * row).astype(BF16)
            acc[k] += jnp.dot(scaled, block, preferred_element_type=F32)
        for i in range(NY):
            wide = x[d, i].astype(F32)
            total += jnp.sum((wide * wide).reshape(COLS // 8, 8, TOK), axis=0)
        return total

    total = lax.fori_loop(0, NZ, share, jnp.zeros((8, TOK), F32))
    mean = jnp.sum(total, axis=0, keepdims=True) * (1.0 / FEATURES)
    inverse[...] = lax.rsqrt(mean + 1e-05)

    def rows(i, carry):
        r = pl.ds(pl.multiple_of(i * 32, 32), 32)
        inv = inverse[...]
        g = acc[0, r, :] * inv
        u = acc[1, r, :] * inv
        b = back[r, :]
        sigma = jax.nn.sigmoid(g)
        swish = g * sigma
        hidden[r, :] = (swish * u).astype(BF16)
        grads[0, r, :] = (b * u * sigma * (1.0 + g * (1.0 - sigma))).astype(BF16)
        grads[1, r, :] = (b * swish).astype(BF16)
        return carry

    lax.fori_loop(0, UNITS // 32, rows, 0)
    for h in range(2):
        own = hidden[:, h * HALF : (h + 1) * HALF]
        pairs = lax.dot_general(own, own, TN, preferred_element_type=F32) * dy_gram[h]
        for s in range(HALF // SEQ):
            part = pairs[s * SEQ : (s + 1) * SEQ, s * SEQ : (s + 1) * SEQ]
            value = jnp.sum(jnp.sum(part, axis=0, keepdims=True), axis=1, keepdims=True)
            i = h * (HALF // SEQ) + s
            down_sq[:, i : i + 1, :] = jnp.broadcast_to(value.reshape(1, 1, 1), (NY, 1, 128))

    def drain(j, carry):
        keep(j).wait()
        return carry

    lax.fori_loop(0, NZ, drain, 0)


def hidden_call(idx, pieces, wg, wu, gain, dy_gram, back):
    return pl.pallas_call(
        hidden_kernel,
        out_shape=(
            jax.ShapeDtypeStruct((NZ, NY, COLS, TOK), BF16),
            jax.ShapeDtypeStruct((UNITS, TOK), BF16),
            jax.ShapeDtypeStruct((1, TOK), F32),
            jax.ShapeDtypeStruct((NY, LOCAL, 128), F32),
            jax.ShapeDtypeStruct((2, UNITS, TOK), BF16),
        ),
        in_specs=[SMEM] + [ANY] * (NZ + 2) + [VMEM] * 3,
        out_specs=(ANY,) + (VMEM,) * 4,
        scratch_shapes=[
            pltpu.VMEM((NZ, NY, COLS, TOK), BF16),
            pltpu.VMEM((NX * NC, UNITS, SHARE), BF16),
            pltpu.VMEM((NX * NC, UNITS, SHARE), BF16),
            pltpu.VMEM((2, UNITS, TOK), F32),
            pltpu.SemaphoreType.DMA((3, NZ)),
            pltpu.SemaphoreType.DMA((NZ,)),
        ],
        compiler_params=params(40),
        cost_estimate=cost(2 * UNITS * TOK * FEATURES, 14 << 20),
        name="hidden",
    )(idx, *pieces, wg, wu, gain, dy_gram, back)


def gain_kernel(grads, inverse, xs, wg, wu, out):
    token = lax.broadcasted_iota(jnp.int32, (TOK, 128), 0)
    column = lax.broadcasted_iota(jnp.int32, (TOK, 128), 1)
    select = jnp.where(token // SEQ == column, 1.0, 0.0).astype(BF16)
    parts, wide = 2, SHARE // 2
    for d in range(2):
        for h in range(parts):
            f = slice(h * wide, (h + 1) * wide)
            normed = lax.dot_general(wg[d, :, f], grads[0], TN, preferred_element_type=F32)
            normed += lax.dot_general(wu[d, :, f], grads[1], TN, preferred_element_type=F32)
            group = wide // COLS
            block = xs[d, h * group : (h + 1) * group].reshape(wide, TOK)
            product = block.astype(F32) * inverse[...] * normed
            high = product.astype(BF16)
            low = (product - high.astype(F32)).astype(BF16)
            total = jnp.dot(high, select, preferred_element_type=F32)
            total += jnp.dot(low, select, preferred_element_type=F32)
            flat = total.T[:LOCAL]
            for k in range(wide // 128):
                tile = h * (wide // 128) + k
                out[d, tile * LOCAL : (tile + 1) * LOCAL, :] = flat[:, k * 128 : (k + 1) * 128]


def gain_call(grads, inverse, xs, wg, wu):
    return pl.pallas_call(
        gain_kernel,
        grid=(NZ // 2,),
        out_shape=jax.ShapeDtypeStruct((NZ, SHARE // 128 * LOCAL, 128), F32),
        in_specs=[
            whole((2, UNITS, TOK)),
            whole((1, TOK)),
            lead((2, NY, COLS, TOK)),
            lead((2, UNITS, SHARE)),
            lead((2, UNITS, SHARE)),
        ],
        out_specs=lead((2, SHARE // 128 * LOCAL, 128)),
        compiler_params=params(32),
        cost_estimate=cost(3 * UNITS * TOK * FEATURES, 9 << 20),
        name="gain_term",
    )(grads, inverse, xs, wg, wu)


def join_kernel(part, gain_part, out):
    total = jnp.sum(part[...], axis=0, keepdims=True)
    out[:, :LOCAL, :] = jnp.broadcast_to(total, (NZ, LOCAL, 128))
    out[:, LOCAL:, :] = gain_part[...]


def join_call(part, gain_part):
    rows = LOCAL + gain_part.shape[1]
    return pl.pallas_call(join_kernel, out_shape=jax.ShapeDtypeStruct((NZ, rows, 128), F32), name="join_parts")(
        part, gain_part
    )


def add_kernel(part, out):
    total = jnp.sum(part[:, LOCAL:, :], axis=0, keepdims=True)
    out[...] = jnp.broadcast_to(total, out.shape)


def add_call(part):
    shape = (NY, part.shape[1] - LOCAL, 128)
    return pl.pallas_call(add_kernel, out_shape=jax.ShapeDtypeStruct(shape, F32), name="add_parts")(part)


def gain_sq_kernel(part, total, square):
    gain = jnp.sum(part[...], axis=0)
    total[...] = gain
    rows = jnp.sum((gain * gain).reshape(SHARE // 128, LOCAL, 128), axis=0)
    value = jnp.sum(rows, axis=1, keepdims=True)
    square[...] = jnp.broadcast_to(value[None], square.shape)


def gain_scale_kernel(idx, part, total, out):
    square = jnp.sum(part[...], axis=0)
    bound = 0.5 * math.sqrt(SEQ * FEATURES)
    scale = jnp.minimum(1.0, bound / (jnp.sqrt(square) + 1e-06)) / SEQS
    rows = total[pl.ds(pl.multiple_of(idx[2] // 2 * LOCAL, LOCAL), LOCAL), :]
    value = jnp.sum(scale * rows, axis=0, keepdims=True)
    out[...] = jnp.broadcast_to(value[None], out.shape)


def grad_kernel(part, hidden, dy, out, scaled):
    @pl.when(pl.program_id(0) == 0)
    def _():
        bound = 0.6 * math.sqrt(SEQ * FF * FEATURES)
        total = jnp.sum(part[:, :LOCAL, :], axis=0)
        scale = jnp.minimum(1.0, bound / (jnp.sqrt(total) + 1e-06)) / SEQS
        first = lax.broadcasted_iota(jnp.int32, (1, 128), 1) < SEQ
        row = jnp.concatenate(
            [jnp.where(first, scale[2 * k : 2 * k + 1], scale[2 * k + 1 : 2 * k + 2]) for k in range(LOCAL // 2)],
            axis=1,
        )
        scaled[...] = (hidden[...].astype(F32) * row).astype(BF16)

    for d in range(2):
        block = dy[d].reshape(SHARE, TOK)
        out[d] = lax.dot_general(scaled[...], block, NT, preferred_element_type=F32).astype(BF16)


def grad_call(part, hidden, dy):
    return pl.pallas_call(
        grad_kernel,
        grid=(NZ // 2,),
        out_shape=jax.ShapeDtypeStruct((NX * NC, UNITS, SHARE), BF16),
        in_specs=[whole(part.shape), whole((UNITS, TOK)), lead((2, NY, COLS, TOK))],
        out_specs=lead((2, UNITS, SHARE)),
        scratch_shapes=[pltpu.VMEM((UNITS, TOK), BF16)],
        compiler_params=params(24),
        cost_estimate=cost(UNITS * TOK * FEATURES, 6 << 20),
        name="grad_down",
    )(part, hidden, dy)


def spread(block, axis, count):
    return lax.all_to_all(
        jnp.broadcast_to(block[None], (count,) + block.shape), axis, split_axis=0, concat_axis=0, tiled=True
    )


def exchange(blocks, axis):
    return lax.all_to_all(blocks, axis, split_axis=0, concat_axis=0, tiled=True)


def ring(block, axis, size):
    shift = lambda k: [(i, (i + k) % size) for i in range(size)]
    up, down = [block], [block]
    for step in range(size // 2):
        up.append(lax.ppermute(up[-1], axis, shift(1)))
        if step < size // 2 - 1:
            down.append(lax.ppermute(down[-1], axis, shift(-1)))
    return up + down[:0:-1]


def body(tokens, gain, cotangent, gate_weight, up_weight, down_weight):
    idx = jnp.stack([lax.axis_index("z"), lax.axis_index("core"), lax.axis_index("y")]).astype(jnp.int32)
    dp = ("x", "core")
    wg = lax.all_gather(gate_weight.T, dp, axis=0)
    wu = lax.all_gather(up_weight.T, dp, axis=0)
    dy_part = spread(cotangent.T, "z", NZ)
    tokens, dy_part = lax.optimization_barrier((tokens, dy_part))
    x_part = spread(tokens.T, "y", NY)
    down_weight, x_part = lax.optimization_barrier((down_weight, x_part))
    dmine = spread(down_weight, "x", NX)
    dy_pieces = ring(dy_part, "y", NY)
    pieces = ring(x_part, "z", NZ)
    dother = lax.ppermute(dmine, "core", [(0, 1), (1, 0)])

    dy, dy_gram = cotangent_call(idx, dy_pieces)
    back = back_call(idx, dy, dmine, dother)
    xs, hidden, inverse, sq_part, grads = hidden_call(
        idx, pieces, wg, wu, gain.reshape(NX * NC, SHARE), dy_gram, back
    )
    part = exchange(sq_part, "y")
    grads, sq_part = lax.optimization_barrier((grads, sq_part))
    gain_part = gain_call(grads, inverse, xs, wg, wu)
    part = exchange(join_call(part, gain_part), "z")
    terms = grad_call(part, hidden, dy)
    part, terms = lax.optimization_barrier((part, terms))
    grad_down = lax.psum_scatter(terms, dp, scatter_dimension=0).astype(F32)

    gain_z, gain_sq = pl.pallas_call(
        gain_sq_kernel,
        out_shape=(
            jax.ShapeDtypeStruct((SHARE // 128 * LOCAL, 128), F32),
            jax.ShapeDtypeStruct((NZ, LOCAL, 128), F32),
        ),
        name="gain_sq",
    )(exchange(add_call(part), "y"))
    gain_local = pl.pallas_call(
        gain_scale_kernel,
        out_shape=jax.ShapeDtypeStruct((NX * NC, 8, 128), F32),
        in_specs=[SMEM, VMEM, VMEM],
        name="gain_scale",
    )(idx, exchange(gain_sq, "z"), gain_z)
    gain_all = jnp.sum(exchange(gain_local, dp)[:, 0], axis=0)
    grad_gain = jnp.where(idx[2] % 2 == 0, gain_all[:COLS], gain_all[COLS:])
    return (grad_down, grad_gain)


def solution(mesh):
    split = Mesh(mesh.devices.reshape(NX, NC, NZ, NY), ("x", "core", "z", "y"))
    dp, tensor = ("x", "core"), ("z", "y")
    in_specs = (P(dp, tensor), P(), P(dp, tensor), P(dp, tensor), P(dp, tensor), P(tensor, dp))
    out_specs = (P(tensor, dp), P(tensor))
    return jax.shard_map(body, mesh=split, in_specs=in_specs, out_specs=out_specs, check_vma=False)
```

```python
import math

import jax
import jax.numpy as jnp
from jax import lax
from jax.experimental import pallas as pl
from jax.experimental.pallas import tpu as pltpu
from jax.sharding import Mesh
from jax.sharding import PartitionSpec as P

FEATURES = 4096
FF = 14336
SEQ = 64
SEQS = 64
NX, NC, NZ, NY = 4, 2, 8, 8
LOCAL = 8
TOK = LOCAL * SEQ
UNITS = FF // (NZ * NY)
SHARE = FEATURES // (NX * NC)
COLS = FEATURES // (NZ * NY)
F32 = jnp.float32
BF16 = jnp.bfloat16

SMEM = pl.BlockSpec(memory_space=pltpu.SMEM)
VMEM = pl.BlockSpec(memory_space=pltpu.VMEM)


def params(mib):
    return pltpu.CompilerParams(vmem_limit_bytes=mib * 1024 * 1024)


def cost(macs, nbytes):
    return pl.CostEstimate(flops=2 * macs, bytes_accessed=nbytes, transcendentals=0)


TN = (((0,), (0,)), ((), ()))
NT = (((1,), (1,)), ((), ()))
HALF = TOK // 2
ANY = pl.BlockSpec(memory_space=pl.ANY)


def whole(shape):
    return pl.BlockSpec(shape, lambda i: (0,) * len(shape))


def lead(shape):
    return pl.BlockSpec(shape, lambda i: (i,) + (0,) * (len(shape) - 1))


def cotangent_kernel(idx, *refs):
    pieces, (dy, gram, held, sems, out_sem) = refs[:NY], refs[NY:]
    y = idx[2]
    for j in range(NY):
        slot = lax.rem(y - j + NY, NY)
        pltpu.make_async_copy(pieces[j], held.at[:, slot], sems.at[j]).start()
    for j in range(NY):
        slot = lax.rem(y - j + NY, NY)
        pltpu.make_async_copy(pieces[j], held.at[:, slot], sems.at[j]).wait()
    keep = pltpu.make_async_copy(held, dy, out_sem)
    keep.start()
    for h in range(2):

        def step(z, acc):
            block = held[z, :, :, h * HALF : (h + 1) * HALF].reshape(SHARE, HALF)
            return acc + lax.dot_general(block, block, TN, preferred_element_type=F32)

        gram[h] = lax.fori_loop(0, NZ, step, jnp.zeros((HALF, HALF), F32))
    keep.wait()


def cotangent_call(idx, pieces):
    return pl.pallas_call(
        cotangent_kernel,
        out_shape=(
            jax.ShapeDtypeStruct((NZ, NY, COLS, TOK), BF16),
            jax.ShapeDtypeStruct((2, HALF, HALF), F32),
        ),
        in_specs=[SMEM] + [ANY] * NY,
        out_specs=(ANY, VMEM),
        scratch_shapes=[
            pltpu.VMEM((NZ, NY, COLS, TOK), BF16),
            pltpu.SemaphoreType.DMA((NY,)),
            pltpu.SemaphoreType.DMA,
        ],
        compiler_params=params(60),
        cost_estimate=cost(TOK * HALF * FEATURES, 9 << 20),
        name="cotangent_gram",
    )(idx, *pieces)


def back_kernel(idx, dy, mine, other, back):
    core = idx[1]

    @pl.when(pl.program_id(0) == 0)
    def _():
        back[...] = jnp.zeros_like(back)

    back[...] += jnp.dot(mine[0], dy[core].reshape(SHARE, TOK), preferred_element_type=F32)
    back[...] += jnp.dot(other[0], dy[1 - core].reshape(SHARE, TOK), preferred_element_type=F32)


def back_call(idx, dy, mine, other):
    return pl.pallas_call(
        back_kernel,
        grid=(NX,),
        out_shape=jax.ShapeDtypeStruct((UNITS, TOK), F32),
        in_specs=[SMEM, lead((2, NY, COLS, TOK)), lead((1, UNITS, SHARE)), lead((1, UNITS, SHARE))],
        out_specs=whole((UNITS, TOK)),
        compiler_params=params(60),
        cost_estimate=cost(UNITS * TOK * FEATURES, 7 << 20),
        name="back",
    )(idx, dy, mine, other)


def hidden_kernel(idx, xs, mine, other, gain, dy_gram, back, hidden, inverse, down_sq, grads, acc, squares):
    step, core = pl.program_id(0), idx[1]

    @pl.when(step == 0)
    def _():
        acc[...] = jnp.zeros_like(acc)
        squares[...] = jnp.zeros_like(squares)

    for ref, d in ((mine, core), (other, 1 - core)):
        row = gain[pl.ds(2 * step + d, 1), :]
        block = xs[d]
        for k in range(2):
            scaled = (ref[0, k].astype(F32) * row).astype(BF16)
            acc[k] += jnp.dot(scaled, block, preferred_element_type=F32)
        for i in range(NY):
            wide = xs[d, i * COLS : (i + 1) * COLS, :].astype(F32)
            squares[...] += jnp.sum((wide * wide).reshape(COLS // 8, 8, TOK), axis=0)

    @pl.when(step == NX - 1)
    def _():
        mean = jnp.sum(squares[...], axis=0, keepdims=True) * (1.0 / FEATURES)
        inverse[...] = lax.rsqrt(mean + 1e-05)

        def rows(i, carry):
            r = pl.ds(pl.multiple_of(i * 32, 32), 32)
            inv = inverse[...]
            g = acc[0, r, :] * inv
            u = acc[1, r, :] * inv
            b = back[r, :]
            sigma = jax.nn.sigmoid(g)
            swish = g * sigma
            hidden[r, :] = (swish * u).astype(BF16)
            grads[0, r, :] = (b * u * sigma * (1.0 + g * (1.0 - sigma))).astype(BF16)
            grads[1, r, :] = (b * swish).astype(BF16)
            return carry

        lax.fori_loop(0, UNITS // 32, rows, 0)
        for h in range(2):
            own = hidden[:, h * HALF : (h + 1) * HALF]
            pairs = lax.dot_general(own, own, TN, preferred_element_type=F32) * dy_gram[h]
            for s in range(HALF // SEQ):
                part = pairs[s * SEQ : (s + 1) * SEQ, s * SEQ : (s + 1) * SEQ]
                value = jnp.sum(jnp.sum(part, axis=0, keepdims=True), axis=1, keepdims=True)
                i = h * (HALF // SEQ) + s
                down_sq[:, i : i + 1, :] = jnp.broadcast_to(value.reshape(1, 1, 1), (NY, 1, 128))


def hidden_call(idx, xs, mine, other, gain, dy_gram, back):
    return pl.pallas_call(
        hidden_kernel,
        grid=(NX,),
        out_shape=(
            jax.ShapeDtypeStruct((UNITS, TOK), BF16),
            jax.ShapeDtypeStruct((1, TOK), F32),
            jax.ShapeDtypeStruct((NY, LOCAL, 128), F32),
            jax.ShapeDtypeStruct((2, UNITS, TOK), BF16),
        ),
        in_specs=[
            SMEM,
            lead((2, SHARE, TOK)),
            lead((1, 2, UNITS, SHARE)),
            lead((1, 2, UNITS, SHARE)),
            whole((NX * NC, SHARE)),
            whole((2, HALF, HALF)),
            whole((UNITS, TOK)),
        ],
        out_specs=(whole((UNITS, TOK)), whole((1, TOK)), whole((NY, LOCAL, 128)), whole((2, UNITS, TOK))),
        scratch_shapes=[pltpu.VMEM((2, UNITS, TOK), F32), pltpu.VMEM((8, TOK), F32)],
        compiler_params=params(60),
        cost_estimate=cost(2 * UNITS * TOK * FEATURES, 14 << 20),
        name="hidden",
    )(idx, xs, mine, other, gain, dy_gram, back)


def gain_kernel(idx, grads, inverse, xs, mine, other, out):
    token = lax.broadcasted_iota(jnp.int32, (TOK, 128), 0)
    column = lax.broadcasted_iota(jnp.int32, (TOK, 128), 1)
    select = jnp.where(token // SEQ == column, 1.0, 0.0).astype(BF16)
    core = idx[1]
    parts, wide = 2, SHARE // 2
    for ref, d in ((mine, core), (other, 1 - core)):
        for h in range(parts):
            f = slice(h * wide, (h + 1) * wide)
            normed = lax.dot_general(ref[0, 0, :, f], grads[0], TN, preferred_element_type=F32)
            normed += lax.dot_general(ref[0, 1, :, f], grads[1], TN, preferred_element_type=F32)
            product = xs[d, f, :].astype(F32) * inverse[...] * normed
            high = product.astype(BF16)
            low = (product - high.astype(F32)).astype(BF16)
            total = jnp.dot(high, select, preferred_element_type=F32)
            total += jnp.dot(low, select, preferred_element_type=F32)
            flat = total.T[:LOCAL]
            for k in range(wide // 128):
                tile = h * (wide // 128) + k
                out[d, tile * LOCAL : (tile + 1) * LOCAL, :] = flat[:, k * 128 : (k + 1) * 128]


def gain_call(idx, grads, inverse, xs, mine, other):
    return pl.pallas_call(
        gain_kernel,
        grid=(NX,),
        out_shape=jax.ShapeDtypeStruct((NZ, SHARE // 128 * LOCAL, 128), F32),
        in_specs=[
            SMEM,
            whole((2, UNITS, TOK)),
            whole((1, TOK)),
            lead((2, SHARE, TOK)),
            lead((1, 2, UNITS, SHARE)),
            lead((1, 2, UNITS, SHARE)),
        ],
        out_specs=lead((2, SHARE // 128 * LOCAL, 128)),
        compiler_params=params(60),
        cost_estimate=cost(3 * UNITS * TOK * FEATURES, 9 << 20),
        name="gain_term",
    )(idx, grads, inverse, xs, mine, other)


def join_kernel(part, gain_part, out):
    total = jnp.sum(part[...], axis=0, keepdims=True)
    out[:, :LOCAL, :] = jnp.broadcast_to(total, (NZ, LOCAL, 128))
    out[:, LOCAL:, :] = gain_part[...]


def join_call(part, gain_part):
    rows = LOCAL + gain_part.shape[1]
    return pl.pallas_call(join_kernel, out_shape=jax.ShapeDtypeStruct((NZ, rows, 128), F32), name="join_parts")(
        part, gain_part
    )


def add_kernel(part, out):
    total = jnp.sum(part[:, LOCAL:, :], axis=0, keepdims=True)
    out[...] = jnp.broadcast_to(total, out.shape)


def add_call(part):
    shape = (NY, part.shape[1] - LOCAL, 128)
    return pl.pallas_call(add_kernel, out_shape=jax.ShapeDtypeStruct(shape, F32), name="add_parts")(part)


def gain_sq_kernel(part, total, square):
    gain = jnp.sum(part[...], axis=0)
    total[...] = gain
    rows = jnp.sum((gain * gain).reshape(SHARE // 128, LOCAL, 128), axis=0)
    value = jnp.sum(rows, axis=1, keepdims=True)
    square[...] = jnp.broadcast_to(value[None], square.shape)


def gain_scale_kernel(idx, part, total, out):
    square = jnp.sum(part[...], axis=0)
    bound = 0.5 * math.sqrt(SEQ * FEATURES)
    scale = jnp.minimum(1.0, bound / (jnp.sqrt(square) + 1e-06)) / SEQS
    rows = total[pl.ds(pl.multiple_of(idx[2] // 2 * LOCAL, LOCAL), LOCAL), :]
    value = jnp.sum(scale * rows, axis=0, keepdims=True)
    out[...] = jnp.broadcast_to(value[None], out.shape)


def grad_kernel(part, hidden, dy, out, scaled):
    @pl.when(pl.program_id(0) == 0)
    def _():
        bound = 0.6 * math.sqrt(SEQ * FF * FEATURES)
        total = jnp.sum(part[:, :LOCAL, :], axis=0)
        scale = jnp.minimum(1.0, bound / (jnp.sqrt(total) + 1e-06)) / SEQS
        first = lax.broadcasted_iota(jnp.int32, (1, 128), 1) < SEQ
        row = jnp.concatenate(
            [jnp.where(first, scale[2 * k : 2 * k + 1], scale[2 * k + 1 : 2 * k + 2]) for k in range(LOCAL // 2)],
            axis=1,
        )
        scaled[...] = (hidden[...].astype(F32) * row).astype(BF16)

    for d in range(2):
        block = dy[d].reshape(SHARE, TOK)
        out[d] = lax.dot_general(scaled[...], block, NT, preferred_element_type=F32).astype(BF16)


def grad_call(part, hidden, dy):
    return pl.pallas_call(
        grad_kernel,
        grid=(NZ // 2,),
        out_shape=jax.ShapeDtypeStruct((NX * NC, UNITS, SHARE), BF16),
        in_specs=[whole(part.shape), whole((UNITS, TOK)), lead((2, NY, COLS, TOK))],
        out_specs=lead((2, UNITS, SHARE)),
        scratch_shapes=[pltpu.VMEM((UNITS, TOK), BF16)],
        compiler_params=params(60),
        cost_estimate=cost(UNITS * TOK * FEATURES, 6 << 20),
        name="grad_down",
    )(part, hidden, dy)


def spread(block, axis, count):
    return lax.all_to_all(
        jnp.broadcast_to(block[None], (count,) + block.shape), axis, split_axis=0, concat_axis=0, tiled=True
    )


def exchange(blocks, axis):
    return lax.all_to_all(blocks, axis, split_axis=0, concat_axis=0, tiled=True)


def ring(block, axis, size):
    shift = lambda k: [(i, (i + k) % size) for i in range(size)]
    up, down = [block], [block]
    for step in range(size // 2):
        up.append(lax.ppermute(up[-1], axis, shift(1)))
        if step < size // 2 - 1:
            down.append(lax.ppermute(down[-1], axis, shift(-1)))
    return up + down[:0:-1]


def body(tokens, gain, cotangent, gate_weight, up_weight, down_weight):
    idx = jnp.stack([lax.axis_index("z"), lax.axis_index("core"), lax.axis_index("y")]).astype(jnp.int32)
    dp = ("x", "core")
    xs = lax.all_gather(tokens.T, ("z", "y"), axis=0, tiled=True).reshape(NZ, SHARE, TOK)
    dy_part = spread(cotangent.T, "z", NZ)
    gate_weight, up_weight, dy_part = lax.optimization_barrier((gate_weight, up_weight, dy_part))
    mine = spread(jnp.stack([gate_weight.T, up_weight.T]), "x", NX)
    down_weight, mine = lax.optimization_barrier((down_weight, mine))
    dmine = spread(down_weight, "x", NX)
    dy_pieces = ring(dy_part, "y", NY)
    swap = [(0, 1), (1, 0)]
    other = lax.ppermute(mine, "core", swap)
    dother = lax.ppermute(dmine, "core", swap)

    dy, dy_gram = cotangent_call(idx, dy_pieces)
    back = back_call(idx, dy, dmine, dother)
    hidden, inverse, sq_part, grads = hidden_call(
        idx, xs, mine, other, gain.reshape(NX * NC, SHARE), dy_gram, back
    )
    part = exchange(sq_part, "y")
    grads, sq_part = lax.optimization_barrier((grads, sq_part))
    gain_part = gain_call(idx, grads, inverse, xs, mine, other)
    part = exchange(join_call(part, gain_part), "z")
    terms = grad_call(part, hidden, dy)
    part, terms = lax.optimization_barrier((part, terms))
    grad_down = lax.psum_scatter(terms, dp, scatter_dimension=0).astype(F32)

    gain_z, gain_sq = pl.pallas_call(
        gain_sq_kernel,
        out_shape=(
            jax.ShapeDtypeStruct((SHARE // 128 * LOCAL, 128), F32),
            jax.ShapeDtypeStruct((NZ, LOCAL, 128), F32),
        ),
        name="gain_sq",
    )(exchange(add_call(part), "y"))
    gain_local = pl.pallas_call(
        gain_scale_kernel,
        out_shape=jax.ShapeDtypeStruct((NX * NC, 8, 128), F32),
        in_specs=[SMEM, VMEM, VMEM],
        name="gain_scale",
    )(idx, exchange(gain_sq, "z"), gain_z)
    gain_all = jnp.sum(exchange(gain_local, dp)[:, 0], axis=0)
    grad_gain = jnp.where(idx[2] % 2 == 0, gain_all[:COLS], gain_all[COLS:])
    return (grad_down, grad_gain)


def solution(mesh):
    split = Mesh(mesh.devices.reshape(NX, NC, NZ, NY), ("x", "core", "z", "y"))
    dp, tensor = ("x", "core"), ("z", "y")
    in_specs = (P(dp, tensor), P(), P(dp, tensor), P(dp, tensor), P(dp, tensor), P(tensor, dp))
    out_specs = (P(tensor, dp), P(tensor))
    return jax.shard_map(body, mesh=split, in_specs=in_specs, out_specs=out_specs, check_vma=False)
```

```python
import math

import jax
import jax.numpy as jnp
from jax import lax
from jax.experimental import pallas as pl
from jax.experimental.pallas import tpu as pltpu
from jax.sharding import Mesh
from jax.sharding import PartitionSpec as P

FEATURES = 4096
FF = 14336
SEQ = 64
SEQS = 64
NX, NC, NZ, NY = 4, 2, 8, 8
LOCAL = 8
TOK = LOCAL * SEQ
UNITS = FF // (NZ * NY)
SHARE = FEATURES // (NX * NC)
COLS = FEATURES // (NZ * NY)
F32 = jnp.float32
BF16 = jnp.bfloat16

SMEM = pl.BlockSpec(memory_space=pltpu.SMEM)
VMEM = pl.BlockSpec(memory_space=pltpu.VMEM)


def params(mib):
    return pltpu.CompilerParams(vmem_limit_bytes=mib * 1024 * 1024)


def cost(macs, nbytes):
    return pl.CostEstimate(flops=2 * macs, bytes_accessed=nbytes, transcendentals=0)


TN = (((0,), (0,)), ((), ()))
NT = (((1,), (1,)), ((), ()))
HALF = TOK // 2
ANY = pl.BlockSpec(memory_space=pl.ANY)


def whole(shape):
    return pl.BlockSpec(shape, lambda i: (0,) * len(shape))


def lead(shape):
    return pl.BlockSpec(shape, lambda i: (i,) + (0,) * (len(shape) - 1))


def rotated(shape):
    return pl.BlockSpec(shape, lambda i, idx: (lax.rem(idx[3] - i + NX, NX),) + (0,) * (len(shape) - 1))


def fixed(shape):
    return pl.BlockSpec(shape, lambda i, idx: (0,) * len(shape))


def weights(first, count):
    return pl.BlockSpec((1, count, UNITS, SHARE), lambda i, idx: (i, first // count, 0, 0))


def cotangent_kernel(idx, *refs):
    pieces, (dy, gram, held, sems, out_sem) = refs[:NY], refs[NY:]
    y = idx[2]
    for j in range(NY):
        slot = lax.rem(y - j + NY, NY)
        pltpu.make_async_copy(pieces[j], held.at[:, slot], sems.at[j]).start()
    for j in range(NY):
        slot = lax.rem(y - j + NY, NY)
        pltpu.make_async_copy(pieces[j], held.at[:, slot], sems.at[j]).wait()
    keep = pltpu.make_async_copy(held, dy, out_sem)
    keep.start()
    for h in range(2):

        def step(z, acc):
            block = held[z, :, :, h * HALF : (h + 1) * HALF].reshape(SHARE, HALF)
            return acc + lax.dot_general(block, block, TN, preferred_element_type=F32)

        gram[h] = lax.fori_loop(0, NZ, step, jnp.zeros((HALF, HALF), F32))
    keep.wait()


def cotangent_call(idx, pieces):
    return pl.pallas_call(
        cotangent_kernel,
        out_shape=(
            jax.ShapeDtypeStruct((NZ, NY, COLS, TOK), BF16),
            jax.ShapeDtypeStruct((2, HALF, HALF), F32),
        ),
        in_specs=[SMEM] + [ANY] * NY,
        out_specs=(ANY, VMEM),
        scratch_shapes=[
            pltpu.VMEM((NZ, NY, COLS, TOK), BF16),
            pltpu.SemaphoreType.DMA((NY,)),
            pltpu.SemaphoreType.DMA,
        ],
        compiler_params=params(60),
        cost_estimate=cost(TOK * HALF * FEATURES, 9 << 20),
        name="cotangent_gram",
    )(idx, *pieces)


def back_kernel(idx, dy, mine, other, back):
    core = idx[1]

    @pl.when(pl.program_id(0) == 0)
    def _():
        back[...] = jnp.zeros_like(back)

    back[...] += jnp.dot(mine[0, 0], dy[core].reshape(SHARE, TOK), preferred_element_type=F32)
    back[...] += jnp.dot(other[0, 0], dy[1 - core].reshape(SHARE, TOK), preferred_element_type=F32)


def back_call(idx, dy, mine, other):
    return pl.pallas_call(
        back_kernel,
        out_shape=jax.ShapeDtypeStruct((UNITS, TOK), F32),
        grid_spec=pltpu.PrefetchScalarGridSpec(
            num_scalar_prefetch=1,
            grid=(NX,),
            in_specs=[rotated((2, NY, COLS, TOK)), weights(2, 1), weights(2, 1)],
            out_specs=fixed((UNITS, TOK)),
        ),
        compiler_params=params(60),
        cost_estimate=cost(UNITS * TOK * FEATURES, 7 << 20),
        name="back",
    )(idx, dy, mine, other)


def hidden_kernel(idx, xs, mine, other, gain, dy_gram, back, hidden, inverse, down_sq, grads, acc, squares):
    step, core = pl.program_id(0), idx[1]
    chip = lax.rem(idx[3] - step + NX, NX)

    @pl.when(step == 0)
    def _():
        acc[...] = jnp.zeros_like(acc)
        squares[...] = jnp.zeros_like(squares)

    for ref, d in ((mine, core), (other, 1 - core)):
        row = gain[pl.ds(2 * chip + d, 1), :]
        block = xs[d]
        for k in range(2):
            scaled = (ref[0, k].astype(F32) * row).astype(BF16)
            acc[k] += jnp.dot(scaled, block, preferred_element_type=F32)
        for i in range(NY):
            wide = xs[d, i * COLS : (i + 1) * COLS, :].astype(F32)
            squares[...] += jnp.sum((wide * wide).reshape(COLS // 8, 8, TOK), axis=0)

    @pl.when(step == NX - 1)
    def _():
        mean = jnp.sum(squares[...], axis=0, keepdims=True) * (1.0 / FEATURES)
        inverse[...] = lax.rsqrt(mean + 1e-05)

        def rows(i, carry):
            r = pl.ds(pl.multiple_of(i * 32, 32), 32)
            inv = inverse[...]
            g = acc[0, r, :] * inv
            u = acc[1, r, :] * inv
            b = back[r, :]
            sigma = jax.nn.sigmoid(g)
            swish = g * sigma
            hidden[r, :] = (swish * u).astype(BF16)
            grads[0, r, :] = (b * u * sigma * (1.0 + g * (1.0 - sigma))).astype(BF16)
            grads[1, r, :] = (b * swish).astype(BF16)
            return carry

        lax.fori_loop(0, UNITS // 32, rows, 0)
        for h in range(2):
            own = hidden[:, h * HALF : (h + 1) * HALF]
            pairs = lax.dot_general(own, own, TN, preferred_element_type=F32) * dy_gram[h]
            for s in range(HALF // SEQ):
                part = pairs[s * SEQ : (s + 1) * SEQ, s * SEQ : (s + 1) * SEQ]
                value = jnp.sum(jnp.sum(part, axis=0, keepdims=True), axis=1, keepdims=True)
                i = h * (HALF // SEQ) + s
                down_sq[:, i : i + 1, :] = jnp.broadcast_to(value.reshape(1, 1, 1), (NY, 1, 128))


def hidden_call(idx, xs, mine, other, gain, dy_gram, back):
    return pl.pallas_call(
        hidden_kernel,
        out_shape=(
            jax.ShapeDtypeStruct((UNITS, TOK), BF16),
            jax.ShapeDtypeStruct((1, TOK), F32),
            jax.ShapeDtypeStruct((NY, LOCAL, 128), F32),
            jax.ShapeDtypeStruct((2, UNITS, TOK), BF16),
        ),
        grid_spec=pltpu.PrefetchScalarGridSpec(
            num_scalar_prefetch=1,
            grid=(NX,),
            in_specs=[
                rotated((2, SHARE, TOK)),
                weights(0, 2),
                weights(0, 2),
                fixed((NX * NC, SHARE)),
                fixed((2, HALF, HALF)),
                fixed((UNITS, TOK)),
            ],
            out_specs=(fixed((UNITS, TOK)), fixed((1, TOK)), fixed((NY, LOCAL, 128)), fixed((2, UNITS, TOK))),
            scratch_shapes=[pltpu.VMEM((2, UNITS, TOK), F32), pltpu.VMEM((8, TOK), F32)],
        ),
        compiler_params=params(60),
        cost_estimate=cost(2 * UNITS * TOK * FEATURES, 14 << 20),
        name="hidden",
    )(idx, xs, mine, other, gain, dy_gram, back)


def gain_kernel(idx, grads, inverse, xs, mine, other, out):
    token = lax.broadcasted_iota(jnp.int32, (TOK, 128), 0)
    column = lax.broadcasted_iota(jnp.int32, (TOK, 128), 1)
    select = jnp.where(token // SEQ == column, 1.0, 0.0).astype(BF16)
    core = idx[1]
    parts, wide = 2, SHARE // 2
    for ref, d in ((mine, core), (other, 1 - core)):
        for h in range(parts):
            f = slice(h * wide, (h + 1) * wide)
            normed = lax.dot_general(ref[0, 0, :, f], grads[0], TN, preferred_element_type=F32)
            normed += lax.dot_general(ref[0, 1, :, f], grads[1], TN, preferred_element_type=F32)
            product = xs[d, f, :].astype(F32) * inverse[...] * normed
            high = product.astype(BF16)
            low = (product - high.astype(F32)).astype(BF16)
            total = jnp.dot(high, select, preferred_element_type=F32)
            total += jnp.dot(low, select, preferred_element_type=F32)
            flat = total.T[:LOCAL]
            for k in range(wide // 128):
                tile = h * (wide // 128) + k
                out[d, tile * LOCAL : (tile + 1) * LOCAL, :] = flat[:, k * 128 : (k + 1) * 128]


def gain_call(idx, grads, inverse, xs, mine, other):
    return pl.pallas_call(
        gain_kernel,
        out_shape=jax.ShapeDtypeStruct((NZ, SHARE // 128 * LOCAL, 128), F32),
        grid_spec=pltpu.PrefetchScalarGridSpec(
            num_scalar_prefetch=1,
            grid=(NX,),
            in_specs=[
                fixed((2, UNITS, TOK)),
                fixed((1, TOK)),
                rotated((2, SHARE, TOK)),
                weights(0, 2),
                weights(0, 2),
            ],
            out_specs=rotated((2, SHARE // 128 * LOCAL, 128)),
        ),
        compiler_params=params(60),
        cost_estimate=cost(3 * UNITS * TOK * FEATURES, 9 << 20),
        name="gain_term",
    )(idx, grads, inverse, xs, mine, other)


def join_kernel(part, gain_part, out):
    total = jnp.sum(part[...], axis=0, keepdims=True)
    out[:, :LOCAL, :] = jnp.broadcast_to(total, (NZ, LOCAL, 128))
    out[:, LOCAL:, :] = gain_part[...]


def join_call(part, gain_part):
    rows = LOCAL + gain_part.shape[1]
    return pl.pallas_call(join_kernel, out_shape=jax.ShapeDtypeStruct((NZ, rows, 128), F32), name="join_parts")(
        part, gain_part
    )


def add_kernel(part, out):
    total = jnp.sum(part[:, LOCAL:, :], axis=0, keepdims=True)
    out[...] = jnp.broadcast_to(total, out.shape)


def add_call(part):
    shape = (NY, part.shape[1] - LOCAL, 128)
    return pl.pallas_call(add_kernel, out_shape=jax.ShapeDtypeStruct(shape, F32), name="add_parts")(part)


def gain_sq_kernel(part, total, square):
    gain = jnp.sum(part[...], axis=0)
    total[...] = gain
    rows = jnp.sum((gain * gain).reshape(SHARE // 128, LOCAL, 128), axis=0)
    value = jnp.sum(rows, axis=1, keepdims=True)
    square[...] = jnp.broadcast_to(value[None], square.shape)


def gain_scale_kernel(idx, part, total, out):
    square = jnp.sum(part[...], axis=0)
    bound = 0.5 * math.sqrt(SEQ * FEATURES)
    scale = jnp.minimum(1.0, bound / (jnp.sqrt(square) + 1e-06)) / SEQS
    rows = total[pl.ds(pl.multiple_of(idx[2] // 2 * LOCAL, LOCAL), LOCAL), :]
    value = jnp.sum(scale * rows, axis=0, keepdims=True)
    out[...] = jnp.broadcast_to(value[None], out.shape)


def grad_kernel(part, hidden, dy, out, scaled):
    @pl.when(pl.program_id(0) == 0)
    def _():
        bound = 0.6 * math.sqrt(SEQ * FF * FEATURES)
        total = jnp.sum(part[:, :LOCAL, :], axis=0)
        scale = jnp.minimum(1.0, bound / (jnp.sqrt(total) + 1e-06)) / SEQS
        first = lax.broadcasted_iota(jnp.int32, (1, 128), 1) < SEQ
        row = jnp.concatenate(
            [jnp.where(first, scale[2 * k : 2 * k + 1], scale[2 * k + 1 : 2 * k + 2]) for k in range(LOCAL // 2)],
            axis=1,
        )
        scaled[...] = (hidden[...].astype(F32) * row).astype(BF16)

    for d in range(2):
        block = dy[d].reshape(SHARE, TOK)
        out[d] = lax.dot_general(scaled[...], block, NT, preferred_element_type=F32).astype(BF16)


def grad_call(part, hidden, dy):
    return pl.pallas_call(
        grad_kernel,
        grid=(NZ // 2,),
        out_shape=jax.ShapeDtypeStruct((NX * NC, UNITS, SHARE), BF16),
        in_specs=[whole(part.shape), whole((UNITS, TOK)), lead((2, NY, COLS, TOK))],
        out_specs=lead((2, UNITS, SHARE)),
        scratch_shapes=[pltpu.VMEM((UNITS, TOK), BF16)],
        compiler_params=params(60),
        cost_estimate=cost(UNITS * TOK * FEATURES, 6 << 20),
        name="grad_down",
    )(part, hidden, dy)


def spread(block, axis, count):
    return lax.all_to_all(
        jnp.broadcast_to(block[None], (count,) + block.shape), axis, split_axis=0, concat_axis=0, tiled=True
    )


def exchange(blocks, axis):
    return lax.all_to_all(blocks, axis, split_axis=0, concat_axis=0, tiled=True)


def ring(block, axis, size):
    shift = lambda k: [(i, (i + k) % size) for i in range(size)]
    up, down = [block], [block]
    for step in range(size // 2):
        up.append(lax.ppermute(up[-1], axis, shift(1)))
        if step < size // 2 - 1:
            down.append(lax.ppermute(down[-1], axis, shift(-1)))
    return up + down[:0:-1]


def body(tokens, gain, cotangent, gate_weight, up_weight, down_weight):
    idx = jnp.stack([lax.axis_index(name) for name in ("z", "core", "y", "x")]).astype(jnp.int32)
    dp = ("x", "core")
    xs = lax.all_gather(tokens.T, ("z", "y"), axis=0, tiled=True).reshape(NZ, SHARE, TOK)
    dy_part = spread(cotangent.T, "z", NZ)
    block = jnp.stack([gate_weight.T, up_weight.T, down_weight])
    block, dy_part = lax.optimization_barrier((block, dy_part))
    turn = lambda k: [(i, (i + k) % NX) for i in range(NX)]
    right = lax.ppermute(block, "x", turn(1))
    left = lax.ppermute(block, "x", turn(-1))
    far = lax.ppermute(right, "x", turn(1))
    mine = jnp.stack([block, right, far, left])
    other = lax.ppermute(mine, "core", [(0, 1), (1, 0)])
    dy_pieces = ring(dy_part, "y", NY)

    dy, dy_gram = cotangent_call(idx, dy_pieces)
    back = back_call(idx, dy, mine, other)
    hidden, inverse, sq_part, grads = hidden_call(
        idx, xs, mine, other, gain.reshape(NX * NC, SHARE), dy_gram, back
    )
    part = exchange(sq_part, "y")
    grads, sq_part = lax.optimization_barrier((grads, sq_part))
    gain_part = gain_call(idx, grads, inverse, xs, mine, other)
    part = exchange(join_call(part, gain_part), "z")
    added = add_call(part)
    part, added = lax.optimization_barrier((part, added))
    terms = grad_call(part, hidden, dy)
    grad_down = lax.psum_scatter(terms, dp, scatter_dimension=0).astype(F32)

    gain_z, gain_sq = pl.pallas_call(
        gain_sq_kernel,
        out_shape=(
            jax.ShapeDtypeStruct((SHARE // 128 * LOCAL, 128), F32),
            jax.ShapeDtypeStruct((NZ, LOCAL, 128), F32),
        ),
        name="gain_sq",
    )(exchange(added, "y"))
    gain_local = pl.pallas_call(
        gain_scale_kernel,
        out_shape=jax.ShapeDtypeStruct((NX * NC, 8, 128), F32),
        in_specs=[SMEM, VMEM, VMEM],
        name="gain_scale",
    )(idx, exchange(gain_sq, "z"), gain_z)
    gain_all = jnp.sum(exchange(gain_local, dp)[:, 0], axis=0)
    grad_gain = jnp.where(idx[2] % 2 == 0, gain_all[:COLS], gain_all[COLS:])
    return (grad_down, grad_gain)


def solution(mesh):
    split = Mesh(mesh.devices.reshape(NX, NC, NZ, NY), ("x", "core", "z", "y"))
    dp, tensor = ("x", "core"), ("z", "y")
    in_specs = (P(dp, tensor), P(), P(dp, tensor), P(dp, tensor), P(dp, tensor), P(tensor, dp))
    out_specs = (P(tensor, dp), P(tensor))
    return jax.shard_map(body, mesh=split, in_specs=in_specs, out_specs=out_specs, check_vma=False)
```

```python
import math

import jax
import jax.numpy as jnp
from jax import lax
from jax.experimental import pallas as pl
from jax.experimental.pallas import tpu as pltpu
from jax.sharding import Mesh
from jax.sharding import PartitionSpec as P

FEATURES = 4096
FF = 14336
SEQ = 64
SEQS = 64
NX, NC, NZ, NY = 4, 2, 8, 8
LOCAL = 8
TOK = LOCAL * SEQ
UNITS = FF // (NZ * NY)
SHARE = FEATURES // (NX * NC)
COLS = FEATURES // (NZ * NY)
F32 = jnp.float32
BF16 = jnp.bfloat16

SMEM = pl.BlockSpec(memory_space=pltpu.SMEM)
VMEM = pl.BlockSpec(memory_space=pltpu.VMEM)


def params(mib):
    return pltpu.CompilerParams(vmem_limit_bytes=mib * 1024 * 1024)


def cost(macs, nbytes):
    return pl.CostEstimate(flops=2 * macs, bytes_accessed=nbytes, transcendentals=0)


TN = (((0,), (0,)), ((), ()))
NT = (((1,), (1,)), ((), ()))
HALF = TOK // 2
ANY = pl.BlockSpec(memory_space=pl.ANY)


def whole(shape):
    return pl.BlockSpec(shape, lambda i: (0,) * len(shape))


def lead(shape):
    return pl.BlockSpec(shape, lambda i: (i,) + (0,) * (len(shape) - 1))


def rotated(shape):
    return pl.BlockSpec(shape, lambda i, idx: (lax.rem(idx[3] - i + NX, NX),) + (0,) * (len(shape) - 1))


def fixed(shape):
    return pl.BlockSpec(shape, lambda i, idx: (0,) * len(shape))


def weights(first, count):
    return pl.BlockSpec((1, count, UNITS, SHARE), lambda i, idx: (i, first // count, 0, 0))


def cotangent_kernel(idx, *refs):
    pieces, (mine, other, dy, gram, back, held, down, sems, down_sems, out_sem) = refs[:NY], refs[NY:]
    core, y, x = idx[1], idx[2], idx[3]

    def incoming(j):
        return pltpu.make_async_copy(pieces[j], held.at[:, lax.rem(y - j + NY, NY)], sems.at[j])

    def weight(which, ref, i):
        return pltpu.make_async_copy(ref.at[i, 2], down.at[which, i], down_sems.at[which, i])

    for j in range(NY):
        incoming(j).start()
    for which, ref in enumerate((mine, other)):
        for i in range(NX):
            weight(which, ref, i).start()
    for j in range(NY):
        incoming(j).wait()
    keep = pltpu.make_async_copy(held, dy, out_sem)
    keep.start()
    for h in range(2):

        def step(z, acc):
            block = held[z, :, :, h * HALF : (h + 1) * HALF].reshape(SHARE, HALF)
            return acc + lax.dot_general(block, block, TN, preferred_element_type=F32)

        gram[h] = lax.fori_loop(0, NZ, step, jnp.zeros((HALF, HALF), F32))
    for which, ref in enumerate((mine, other)):
        for i in range(NX):
            weight(which, ref, i).wait()
    back[...] = jnp.zeros_like(back)

    def share(i, carry):
        chip = lax.rem(x - i + NX, NX)
        for which, d in ((0, core), (1, 1 - core)):
            block = held[2 * chip + d].reshape(SHARE, TOK)
            back[...] += jnp.dot(down[which, i], block, preferred_element_type=F32)
        return carry

    lax.fori_loop(0, NX, share, 0)
    keep.wait()


def cotangent_call(idx, pieces, mine, other):
    return pl.pallas_call(
        cotangent_kernel,
        out_shape=(
            jax.ShapeDtypeStruct((NZ, NY, COLS, TOK), BF16),
            jax.ShapeDtypeStruct((2, HALF, HALF), F32),
            jax.ShapeDtypeStruct((UNITS, TOK), F32),
        ),
        in_specs=[SMEM] + [ANY] * (NY + 2),
        out_specs=(ANY, VMEM, VMEM),
        scratch_shapes=[
            pltpu.VMEM((NZ, NY, COLS, TOK), BF16),
            pltpu.VMEM((2, NX, UNITS, SHARE), BF16),
            pltpu.SemaphoreType.DMA((NY,)),
            pltpu.SemaphoreType.DMA((2, NX)),
            pltpu.SemaphoreType.DMA,
        ],
        compiler_params=params(60),
        cost_estimate=cost((UNITS + HALF) * TOK * FEATURES, 11 << 20),
        name="cotangent",
    )(idx, *pieces, mine, other)


def hidden_kernel(idx, xs, mine, other, gain, dy_gram, back, hidden, inverse, down_sq, grads, acc, squares):
    step, core = pl.program_id(0), idx[1]
    chip = lax.rem(idx[3] - step + NX, NX)

    @pl.when(step == 0)
    def _():
        acc[...] = jnp.zeros_like(acc)
        squares[...] = jnp.zeros_like(squares)

    for ref, d in ((mine, core), (other, 1 - core)):
        row = gain[pl.ds(2 * chip + d, 1), :]
        block = xs[d]
        for k in range(2):
            scaled = (ref[0, k].astype(F32) * row).astype(BF16)
            acc[k] += jnp.dot(scaled, block, preferred_element_type=F32)
        for i in range(NY):
            wide = xs[d, i * COLS : (i + 1) * COLS, :].astype(F32)
            squares[...] += jnp.sum((wide * wide).reshape(COLS // 8, 8, TOK), axis=0)

    @pl.when(step == NX - 1)
    def _():
        mean = jnp.sum(squares[...], axis=0, keepdims=True) * (1.0 / FEATURES)
        inverse[...] = lax.rsqrt(mean + 1e-05)

        def rows(i, carry):
            r = pl.ds(pl.multiple_of(i * 32, 32), 32)
            inv = inverse[...]
            g = acc[0, r, :] * inv
            u = acc[1, r, :] * inv
            b = back[r, :]
            sigma = jax.nn.sigmoid(g)
            swish = g * sigma
            hidden[r, :] = (swish * u).astype(BF16)
            grads[0, r, :] = (b * u * sigma * (1.0 + g * (1.0 - sigma))).astype(BF16)
            grads[1, r, :] = (b * swish).astype(BF16)
            return carry

        lax.fori_loop(0, UNITS // 32, rows, 0)
        for h in range(2):
            own = hidden[:, h * HALF : (h + 1) * HALF]
            pairs = lax.dot_general(own, own, TN, preferred_element_type=F32) * dy_gram[h]
            for s in range(HALF // SEQ):
                part = pairs[s * SEQ : (s + 1) * SEQ, s * SEQ : (s + 1) * SEQ]
                value = jnp.sum(jnp.sum(part, axis=0, keepdims=True), axis=1, keepdims=True)
                i = h * (HALF // SEQ) + s
                down_sq[:, i : i + 1, :] = jnp.broadcast_to(value.reshape(1, 1, 1), (NY, 1, 128))


def hidden_call(idx, xs, mine, other, gain, dy_gram, back):
    return pl.pallas_call(
        hidden_kernel,
        out_shape=(
            jax.ShapeDtypeStruct((UNITS, TOK), BF16),
            jax.ShapeDtypeStruct((1, TOK), F32),
            jax.ShapeDtypeStruct((NY, LOCAL, 128), F32),
            jax.ShapeDtypeStruct((2, UNITS, TOK), BF16),
        ),
        grid_spec=pltpu.PrefetchScalarGridSpec(
            num_scalar_prefetch=1,
            grid=(NX,),
            in_specs=[
                rotated((2, SHARE, TOK)),
                weights(0, 2),
                weights(0, 2),
                fixed((NX * NC, SHARE)),
                fixed((2, HALF, HALF)),
                fixed((UNITS, TOK)),
            ],
            out_specs=(fixed((UNITS, TOK)), fixed((1, TOK)), fixed((NY, LOCAL, 128)), fixed((2, UNITS, TOK))),
            scratch_shapes=[pltpu.VMEM((2, UNITS, TOK), F32), pltpu.VMEM((8, TOK), F32)],
        ),
        compiler_params=params(60),
        cost_estimate=cost(2 * UNITS * TOK * FEATURES, 14 << 20),
        name="hidden",
    )(idx, xs, mine, other, gain, dy_gram, back)


def gain_kernel(idx, grads, inverse, xs, mine, other, out):
    token = lax.broadcasted_iota(jnp.int32, (TOK, 128), 0)
    column = lax.broadcasted_iota(jnp.int32, (TOK, 128), 1)
    select = jnp.where(token // SEQ == column, 1.0, 0.0).astype(BF16)
    core = idx[1]
    parts, wide = 2, SHARE // 2
    for ref, d in ((mine, core), (other, 1 - core)):
        for h in range(parts):
            f = slice(h * wide, (h + 1) * wide)
            normed = lax.dot_general(ref[0, 0, :, f], grads[0], TN, preferred_element_type=F32)
            normed += lax.dot_general(ref[0, 1, :, f], grads[1], TN, preferred_element_type=F32)
            product = xs[d, f, :].astype(F32) * inverse[...] * normed
            high = product.astype(BF16)
            low = (product - high.astype(F32)).astype(BF16)
            total = jnp.dot(high, select, preferred_element_type=F32)
            total += jnp.dot(low, select, preferred_element_type=F32)
            flat = total.T[:LOCAL]
            for k in range(wide // 128):
                tile = h * (wide // 128) + k
                out[d, tile * LOCAL : (tile + 1) * LOCAL, :] = flat[:, k * 128 : (k + 1) * 128]


def gain_call(idx, grads, inverse, xs, mine, other):
    return pl.pallas_call(
        gain_kernel,
        out_shape=jax.ShapeDtypeStruct((NZ, SHARE // 128 * LOCAL, 128), F32),
        grid_spec=pltpu.PrefetchScalarGridSpec(
            num_scalar_prefetch=1,
            grid=(NX,),
            in_specs=[
                fixed((2, UNITS, TOK)),
                fixed((1, TOK)),
                rotated((2, SHARE, TOK)),
                weights(0, 2),
                weights(0, 2),
            ],
            out_specs=rotated((2, SHARE // 128 * LOCAL, 128)),
        ),
        compiler_params=params(60),
        cost_estimate=cost(3 * UNITS * TOK * FEATURES, 9 << 20),
        name="gain_term",
    )(idx, grads, inverse, xs, mine, other)


def join_kernel(part, gain_part, out):
    total = jnp.sum(part[...], axis=0, keepdims=True)
    out[:, :LOCAL, :] = jnp.broadcast_to(total, (NZ, LOCAL, 128))
    out[:, LOCAL:, :] = gain_part[...]


def join_call(part, gain_part):
    rows = LOCAL + gain_part.shape[1]
    return pl.pallas_call(join_kernel, out_shape=jax.ShapeDtypeStruct((NZ, rows, 128), F32), name="join_parts")(
        part, gain_part
    )


def gain_sq_kernel(part, total, square):
    gain = jnp.sum(part[...], axis=0)
    total[...] = gain
    rows = jnp.sum((gain * gain).reshape(SHARE // 128, LOCAL, 128), axis=0)
    value = jnp.sum(rows, axis=1, keepdims=True)
    square[...] = jnp.broadcast_to(value[None], square.shape)


def gain_scale_kernel(idx, part, total, out):
    square = jnp.sum(part[...], axis=0)
    bound = 0.5 * math.sqrt(SEQ * FEATURES)
    scale = jnp.minimum(1.0, bound / (jnp.sqrt(square) + 1e-06)) / SEQS
    rows = total[pl.ds(pl.multiple_of(idx[2] // 2 * LOCAL, LOCAL), LOCAL), :]
    value = jnp.sum(scale * rows, axis=0, keepdims=True)
    out[...] = jnp.broadcast_to(value[None], out.shape)


def grad_kernel(part, hidden, dy, out, added, scaled):
    @pl.when(pl.program_id(0) == 0)
    def _():
        bound = 0.6 * math.sqrt(SEQ * FF * FEATURES)
        total = jnp.sum(part[:, :LOCAL, :], axis=0)
        scale = jnp.minimum(1.0, bound / (jnp.sqrt(total) + 1e-06)) / SEQS
        first = lax.broadcasted_iota(jnp.int32, (1, 128), 1) < SEQ
        row = jnp.concatenate(
            [jnp.where(first, scale[2 * k : 2 * k + 1], scale[2 * k + 1 : 2 * k + 2]) for k in range(LOCAL // 2)],
            axis=1,
        )
        scaled[...] = (hidden[...].astype(F32) * row).astype(BF16)
        gain = jnp.sum(part[:, LOCAL:, :], axis=0, keepdims=True)
        added[...] = jnp.broadcast_to(gain, added.shape)

    for d in range(2):
        block = dy[d].reshape(SHARE, TOK)
        out[d] = lax.dot_general(scaled[...], block, NT, preferred_element_type=F32).astype(BF16)


def grad_call(part, hidden, dy):
    gain_shape = (NY, part.shape[1] - LOCAL, 128)
    return pl.pallas_call(
        grad_kernel,
        grid=(NZ // 2,),
        out_shape=(
            jax.ShapeDtypeStruct((NX * NC, UNITS, SHARE), BF16),
            jax.ShapeDtypeStruct(gain_shape, F32),
        ),
        in_specs=[whole(part.shape), whole((UNITS, TOK)), lead((2, NY, COLS, TOK))],
        out_specs=(lead((2, UNITS, SHARE)), whole(gain_shape)),
        scratch_shapes=[pltpu.VMEM((UNITS, TOK), BF16)],
        compiler_params=params(60),
        cost_estimate=cost(UNITS * TOK * FEATURES, 6 << 20),
        name="grad_down",
    )(part, hidden, dy)


def spread(block, axis, count):
    return lax.all_to_all(
        jnp.broadcast_to(block[None], (count,) + block.shape), axis, split_axis=0, concat_axis=0, tiled=True
    )


def exchange(blocks, axis):
    return lax.all_to_all(blocks, axis, split_axis=0, concat_axis=0, tiled=True)


def turn(block, axis, k):
    size = lax.axis_size(axis)
    return lax.ppermute(block, axis, [(i, (i + k) % size) for i in range(size)])


def body(tokens, gain, cotangent, gate_weight, up_weight, down_weight):
    idx = jnp.stack([lax.axis_index(name) for name in ("z", "core", "y", "x")]).astype(jnp.int32)
    dp = ("x", "core")
    xs = lax.all_gather(tokens.T, ("z", "y"), axis=0, tiled=True).reshape(NZ, SHARE, TOK)
    dy_part = spread(cotangent.T, "z", NZ)
    block = jnp.stack([gate_weight.T, up_weight.T, down_weight])
    block, dy_part = lax.optimization_barrier((block, dy_part))
    stage = lax.optimization_barrier(
        (turn(dy_part, "y", 1), turn(dy_part, "y", -1), turn(block, "x", 1), turn(block, "x", -1))
    )
    up_1, down_1, right, left = stage
    up_2, down_2, far = lax.optimization_barrier((turn(up_1, "y", 1), turn(down_1, "y", -1), turn(right, "x", 1)))
    up_3, down_3 = lax.optimization_barrier((turn(up_2, "y", 1), turn(down_2, "y", -1)))
    mine = jnp.stack([block, right, far, left])
    other = turn(mine, "core", 1)
    up_4 = turn(up_3, "y", 1)
    dy_pieces = [dy_part, up_1, up_2, up_3, up_4, down_3, down_2, down_1]

    dy, dy_gram, back = cotangent_call(idx, dy_pieces, mine, other)
    hidden, inverse, sq_part, grads = hidden_call(
        idx, xs, mine, other, gain.reshape(NX * NC, SHARE), dy_gram, back
    )
    part = exchange(sq_part, "y")
    grads, sq_part = lax.optimization_barrier((grads, sq_part))
    gain_part = gain_call(idx, grads, inverse, xs, mine, other)
    part = exchange(join_call(part, gain_part), "z")
    terms, added = grad_call(part, hidden, dy)
    grad_down = lax.psum_scatter(terms, dp, scatter_dimension=0).astype(F32)

    gain_z, gain_sq = pl.pallas_call(
        gain_sq_kernel,
        out_shape=(
            jax.ShapeDtypeStruct((SHARE // 128 * LOCAL, 128), F32),
            jax.ShapeDtypeStruct((NZ, LOCAL, 128), F32),
        ),
        name="gain_sq",
    )(exchange(added, "y"))
    gain_local = pl.pallas_call(
        gain_scale_kernel,
        out_shape=jax.ShapeDtypeStruct((NX * NC, 8, 128), F32),
        in_specs=[SMEM, VMEM, VMEM],
        name="gain_scale",
    )(idx, exchange(gain_sq, "z"), gain_z)
    gain_all = jnp.sum(exchange(gain_local, dp)[:, 0], axis=0)
    grad_gain = jnp.where(idx[2] % 2 == 0, gain_all[:COLS], gain_all[COLS:])
    return (grad_down, grad_gain)


def solution(mesh):
    split = Mesh(mesh.devices.reshape(NX, NC, NZ, NY), ("x", "core", "z", "y"))
    dp, tensor = ("x", "core"), ("z", "y")
    in_specs = (P(dp, tensor), P(), P(dp, tensor), P(dp, tensor), P(dp, tensor), P(tensor, dp))
    out_specs = (P(tensor, dp), P(tensor))
    return jax.shard_map(body, mesh=split, in_specs=in_specs, out_specs=out_specs, check_vma=False)
```

```python
import math

import jax
import jax.numpy as jnp
from jax import lax
from jax.experimental import pallas as pl
from jax.experimental.pallas import tpu as pltpu
from jax.sharding import Mesh
from jax.sharding import PartitionSpec as P

FEATURES = 4096
FF = 14336
SEQ = 64
SEQS = 64
NX, NC, NZ, NY = 4, 2, 8, 8
LOCAL = 8
TOK = LOCAL * SEQ
UNITS = FF // (NZ * NY)
SHARE = FEATURES // (NX * NC)
COLS = FEATURES // (NZ * NY)
F32 = jnp.float32
BF16 = jnp.bfloat16

SMEM = pl.BlockSpec(memory_space=pltpu.SMEM)
VMEM = pl.BlockSpec(memory_space=pltpu.VMEM)


def params(mib):
    return pltpu.CompilerParams(vmem_limit_bytes=mib * 1024 * 1024)


def cost(macs, nbytes):
    return pl.CostEstimate(flops=2 * macs, bytes_accessed=nbytes, transcendentals=0)


TN = (((0,), (0,)), ((), ()))
NT = (((1,), (1,)), ((), ()))
HALF = TOK // 2
ANY = pl.BlockSpec(memory_space=pl.ANY)


def whole(shape):
    return pl.BlockSpec(shape, lambda i: (0,) * len(shape))


def lead(shape):
    return pl.BlockSpec(shape, lambda i: (i,) + (0,) * (len(shape) - 1))


def cotangent_kernel(idx, *refs):
    pieces, (weight, dy, gram, back, held, down, sems, down_sem, out_sem) = refs[:NY], refs[NY:]
    y = idx[1]

    def incoming(j):
        return pltpu.make_async_copy(pieces[j], held.at[:, lax.rem(y - j + NY, NY)], sems.at[j])

    fetch = pltpu.make_async_copy(weight.at[:, 2], down, down_sem)
    for j in range(NY):
        incoming(j).start()
    fetch.start()
    for j in range(NY):
        incoming(j).wait()
    keep = pltpu.make_async_copy(held, dy, out_sem)
    keep.start()
    for h in range(2):

        def step(z, acc):
            block = held[z, :, :, h * HALF : (h + 1) * HALF].reshape(SHARE, HALF)
            return acc + lax.dot_general(block, block, TN, preferred_element_type=F32)

        gram[h] = lax.fori_loop(0, NZ, step, jnp.zeros((HALF, HALF), F32))
    fetch.wait()
    back[...] = jnp.zeros_like(back)

    def share(d, carry):
        back[...] += jnp.dot(down[d], held[d].reshape(SHARE, TOK), preferred_element_type=F32)
        return carry

    lax.fori_loop(0, NX * NC, share, 0)
    keep.wait()


def cotangent_call(idx, pieces, weight):
    return pl.pallas_call(
        cotangent_kernel,
        out_shape=(
            jax.ShapeDtypeStruct((NZ, NY, COLS, TOK), BF16),
            jax.ShapeDtypeStruct((2, HALF, HALF), F32),
            jax.ShapeDtypeStruct((UNITS, TOK), F32),
        ),
        in_specs=[SMEM] + [ANY] * (NY + 1),
        out_specs=(ANY, VMEM, VMEM),
        scratch_shapes=[
            pltpu.VMEM((NZ, NY, COLS, TOK), BF16),
            pltpu.VMEM((NX * NC, UNITS, SHARE), BF16),
            pltpu.SemaphoreType.DMA((NY,)),
            pltpu.SemaphoreType.DMA,
            pltpu.SemaphoreType.DMA,
        ],
        compiler_params=params(60),
        cost_estimate=cost((UNITS + HALF) * TOK * FEATURES, 11 << 20),
        name="cotangent",
    )(idx, *pieces, weight)


def hidden_kernel(idx, *refs):
    pieces, (weight, gain, dy_gram, back, xs, hidden, inverse, down_sq, grads) = refs[:NZ], refs[NZ : NZ + 9]
    x, held, acc, sems, weight_sems, out_sems = refs[NZ + 9 :]
    z, y = idx[0], idx[1]

    def place(j):
        return lax.rem(z - j + NZ, NZ)

    def fetch(j):
        d = place(j)
        return pltpu.make_async_copy(weight.at[d, :2], held.at[d], weight_sems.at[j])

    def keep(j):
        d = place(j)
        return pltpu.make_async_copy(x.at[d], xs.at[d], out_sems.at[j])

    for j in range(NZ):
        for i in range(NY):
            slot = lax.rem(y - i + NY, NY)
            pltpu.make_async_copy(pieces[j].at[i], x.at[place(j), slot], sems.at[j]).start()
        fetch(j).start()
    acc[...] = jnp.zeros_like(acc)

    def share(j, total):
        d = place(j)
        pltpu.make_async_copy(pieces[0], x.at[d], sems.at[j]).wait()
        fetch(j).wait()
        keep(j).start()
        row = gain[pl.ds(d, 1), :]
        block = x[d].reshape(SHARE, TOK)
        for k in range(2):
            scaled = (held[d, k].astype(F32) * row).astype(BF16)
            acc[k] += jnp.dot(scaled, block, preferred_element_type=F32)
        for i in range(NY):
            wide = x[d, i].astype(F32)
            total += jnp.sum((wide * wide).reshape(COLS // 8, 8, TOK), axis=0)
        return total

    total = lax.fori_loop(0, NZ, share, jnp.zeros((8, TOK), F32))
    mean = jnp.sum(total, axis=0, keepdims=True) * (1.0 / FEATURES)
    inverse[...] = lax.rsqrt(mean + 1e-05)

    def rows(i, carry):
        r = pl.ds(pl.multiple_of(i * 32, 32), 32)
        inv = inverse[...]
        g = acc[0, r, :] * inv
        u = acc[1, r, :] * inv
        b = back[r, :]
        sigma = jax.nn.sigmoid(g)
        swish = g * sigma
        hidden[r, :] = (swish * u).astype(BF16)
        grads[0, r, :] = (b * u * sigma * (1.0 + g * (1.0 - sigma))).astype(BF16)
        grads[1, r, :] = (b * swish).astype(BF16)
        return carry

    lax.fori_loop(0, UNITS // 32, rows, 0)
    for h in range(2):
        own = hidden[:, h * HALF : (h + 1) * HALF]
        pairs = lax.dot_general(own, own, TN, preferred_element_type=F32) * dy_gram[h]
        for s in range(HALF // SEQ):
            part = pairs[s * SEQ : (s + 1) * SEQ, s * SEQ : (s + 1) * SEQ]
            value = jnp.sum(jnp.sum(part, axis=0, keepdims=True), axis=1, keepdims=True)
            i = h * (HALF // SEQ) + s
            down_sq[:, i : i + 1, :] = jnp.broadcast_to(value.reshape(1, 1, 1), (NY, 1, 128))

    def drain(j, carry):
        keep(j).wait()
        return carry

    lax.fori_loop(0, NZ, drain, 0)


def hidden_call(idx, pieces, weight, gain, dy_gram, back):
    return pl.pallas_call(
        hidden_kernel,
        out_shape=(
            jax.ShapeDtypeStruct((NZ, NY, COLS, TOK), BF16),
            jax.ShapeDtypeStruct((UNITS, TOK), BF16),
            jax.ShapeDtypeStruct((1, TOK), F32),
            jax.ShapeDtypeStruct((NY, LOCAL, 128), F32),
            jax.ShapeDtypeStruct((2, UNITS, TOK), BF16),
        ),
        in_specs=[SMEM] + [ANY] * (NZ + 1) + [VMEM] * 3,
        out_specs=(ANY,) + (VMEM,) * 4,
        scratch_shapes=[
            pltpu.VMEM((NZ, NY, COLS, TOK), BF16),
            pltpu.VMEM((NX * NC, 2, UNITS, SHARE), BF16),
            pltpu.VMEM((2, UNITS, TOK), F32),
            pltpu.SemaphoreType.DMA((NZ,)),
            pltpu.SemaphoreType.DMA((NZ,)),
            pltpu.SemaphoreType.DMA((NZ,)),
        ],
        compiler_params=params(60),
        cost_estimate=cost(2 * UNITS * TOK * FEATURES, 14 << 20),
        name="hidden",
    )(idx, *pieces, weight, gain, dy_gram, back)


def gain_kernel(grads, inverse, xs, weight, out):
    token = lax.broadcasted_iota(jnp.int32, (TOK, 128), 0)
    column = lax.broadcasted_iota(jnp.int32, (TOK, 128), 1)
    select = jnp.where(token // SEQ == column, 1.0, 0.0).astype(BF16)
    parts, wide = 2, SHARE // 2
    for d in range(2):
        for h in range(parts):
            f = slice(h * wide, (h + 1) * wide)
            normed = lax.dot_general(weight[d, 0, :, f], grads[0], TN, preferred_element_type=F32)
            normed += lax.dot_general(weight[d, 1, :, f], grads[1], TN, preferred_element_type=F32)
            group = wide // COLS
            block = xs[d, h * group : (h + 1) * group].reshape(wide, TOK)
            product = block.astype(F32) * inverse[...] * normed
            high = product.astype(BF16)
            low = (product - high.astype(F32)).astype(BF16)
            total = jnp.dot(high, select, preferred_element_type=F32)
            total += jnp.dot(low, select, preferred_element_type=F32)
            flat = total.T[:LOCAL]
            for k in range(wide // 128):
                tile = h * (wide // 128) + k
                out[d, tile * LOCAL : (tile + 1) * LOCAL, :] = flat[:, k * 128 : (k + 1) * 128]


def gain_call(grads, inverse, xs, weight):
    return pl.pallas_call(
        gain_kernel,
        grid=(NZ // 2,),
        out_shape=jax.ShapeDtypeStruct((NZ, SHARE // 128 * LOCAL, 128), F32),
        in_specs=[
            whole((2, UNITS, TOK)),
            whole((1, TOK)),
            lead((2, NY, COLS, TOK)),
            lead((2, 2, UNITS, SHARE)),
        ],
        out_specs=lead((2, SHARE // 128 * LOCAL, 128)),
        compiler_params=params(60),
        cost_estimate=cost(3 * UNITS * TOK * FEATURES, 9 << 20),
        name="gain_term",
    )(grads, inverse, xs, weight)


def join_kernel(part, gain_part, out):
    total = jnp.sum(part[...], axis=0, keepdims=True)
    out[:, :LOCAL, :] = jnp.broadcast_to(total, (NZ, LOCAL, 128))
    out[:, LOCAL:, :] = gain_part[...]


def join_call(part, gain_part):
    rows = LOCAL + gain_part.shape[1]
    return pl.pallas_call(join_kernel, out_shape=jax.ShapeDtypeStruct((NZ, rows, 128), F32), name="join_parts")(
        part, gain_part
    )


def gain_sq_kernel(part, total, square):
    gain = jnp.sum(part[...], axis=0)
    total[...] = gain
    rows = jnp.sum((gain * gain).reshape(SHARE // 128, LOCAL, 128), axis=0)
    value = jnp.sum(rows, axis=1, keepdims=True)
    square[...] = jnp.broadcast_to(value[None], square.shape)


def gain_scale_kernel(idx, part, total, out):
    square = jnp.sum(part[...], axis=0)
    bound = 0.5 * math.sqrt(SEQ * FEATURES)
    scale = jnp.minimum(1.0, bound / (jnp.sqrt(square) + 1e-06)) / SEQS
    rows = total[pl.ds(pl.multiple_of(idx[1] // 2 * LOCAL, LOCAL), LOCAL), :]
    value = jnp.sum(scale * rows, axis=0, keepdims=True)
    out[...] = jnp.broadcast_to(value[None], out.shape)


def grad_kernel(part, hidden, dy, out, added, scaled):
    @pl.when(pl.program_id(0) == 0)
    def _():
        bound = 0.6 * math.sqrt(SEQ * FF * FEATURES)
        total = jnp.sum(part[:, :LOCAL, :], axis=0)
        scale = jnp.minimum(1.0, bound / (jnp.sqrt(total) + 1e-06)) / SEQS
        first = lax.broadcasted_iota(jnp.int32, (1, 128), 1) < SEQ
        row = jnp.concatenate(
            [jnp.where(first, scale[2 * k : 2 * k + 1], scale[2 * k + 1 : 2 * k + 2]) for k in range(LOCAL // 2)],
            axis=1,
        )
        scaled[...] = (hidden[...].astype(F32) * row).astype(BF16)
        gain = jnp.sum(part[:, LOCAL:, :], axis=0, keepdims=True)
        added[...] = jnp.broadcast_to(gain, added.shape)

    for d in range(2):
        block = dy[d].reshape(SHARE, TOK)
        out[d] = lax.dot_general(scaled[...], block, NT, preferred_element_type=F32).astype(BF16)


def grad_call(part, hidden, dy):
    gain_shape = (NY, part.shape[1] - LOCAL, 128)
    return pl.pallas_call(
        grad_kernel,
        grid=(NZ // 2,),
        out_shape=(
            jax.ShapeDtypeStruct((NX * NC, UNITS, SHARE), BF16),
            jax.ShapeDtypeStruct(gain_shape, F32),
        ),
        in_specs=[whole(part.shape), whole((UNITS, TOK)), lead((2, NY, COLS, TOK))],
        out_specs=(lead((2, UNITS, SHARE)), whole(gain_shape)),
        scratch_shapes=[pltpu.VMEM((UNITS, TOK), BF16)],
        compiler_params=params(60),
        cost_estimate=cost(UNITS * TOK * FEATURES, 6 << 20),
        name="grad_down",
    )(part, hidden, dy)


def spread(block, axis, count):
    return lax.all_to_all(
        jnp.broadcast_to(block[None], (count,) + block.shape), axis, split_axis=0, concat_axis=0, tiled=True
    )


def exchange(blocks, axis):
    return lax.all_to_all(blocks, axis, split_axis=0, concat_axis=0, tiled=True)


def ring(block, axis, size):
    turn = lambda part, k: lax.ppermute(part, axis, [(i, (i + k) % size) for i in range(size)])
    up, down = [block], [block]
    for step in range(size // 2):
        up.append(turn(up[-1], 1))
        if step < size // 2 - 1:
            down.append(turn(down[-1], -1))
    return up + down[:0:-1]


def body(tokens, gain, cotangent, gate_weight, up_weight, down_weight):
    idx = jnp.stack([lax.axis_index("z"), lax.axis_index("y")]).astype(jnp.int32)
    dp = ("x", "core")
    weight = lax.all_gather(jnp.stack([gate_weight.T, up_weight.T, down_weight]), dp, axis=0)
    dy_pieces = ring(spread(cotangent.T, "z", NZ), "y", NY)
    pieces = ring(jnp.stack(ring(tokens.T, "y", NY)), "z", NZ)

    dy, dy_gram, back = cotangent_call(idx, dy_pieces, weight)
    xs, hidden, inverse, sq_part, grads = hidden_call(
        idx, pieces, weight, gain.reshape(NX * NC, SHARE), dy_gram, back
    )
    part = exchange(sq_part, "y")
    grads, sq_part = lax.optimization_barrier((grads, sq_part))
    gain_part = gain_call(grads, inverse, xs, weight)
    part = exchange(join_call(part, gain_part), "z")
    terms, added = grad_call(part, hidden, dy)
    grad_down = lax.psum_scatter(terms, dp, scatter_dimension=0).astype(F32)

    gain_z, gain_sq = pl.pallas_call(
        gain_sq_kernel,
        out_shape=(
            jax.ShapeDtypeStruct((SHARE // 128 * LOCAL, 128), F32),
            jax.ShapeDtypeStruct((NZ, LOCAL, 128), F32),
        ),
        name="gain_sq",
    )(exchange(added, "y"))
    gain_local = pl.pallas_call(
        gain_scale_kernel,
        out_shape=jax.ShapeDtypeStruct((NX * NC, 8, 128), F32),
        in_specs=[SMEM, VMEM, VMEM],
        name="gain_scale",
    )(idx, exchange(gain_sq, "z"), gain_z)
    gain_all = jnp.sum(exchange(gain_local, dp)[:, 0], axis=0)
    grad_gain = jnp.where(idx[1] % 2 == 0, gain_all[:COLS], gain_all[COLS:])
    return (grad_down, grad_gain)


def solution(mesh):
    split = Mesh(mesh.devices.reshape(NX, NC, NZ, NY), ("x", "core", "z", "y"))
    dp, tensor = ("x", "core"), ("z", "y")
    in_specs = (P(dp, tensor), P(), P(dp, tensor), P(dp, tensor), P(dp, tensor), P(tensor, dp))
    out_specs = (P(tensor, dp), P(tensor))
    return jax.shard_map(body, mesh=split, in_specs=in_specs, out_specs=out_specs, check_vma=False)
```

```python
import math

import jax
import jax.numpy as jnp
from jax import lax
from jax.experimental import pallas as pl
from jax.experimental.pallas import tpu as pltpu
from jax.sharding import Mesh
from jax.sharding import PartitionSpec as P

FEATURES = 4096
FF = 14336
SEQ = 64
SEQS = 64
NX, NC, NZ, NY = 4, 2, 8, 8
LOCAL = 8
TOK = LOCAL * SEQ
UNITS = FF // (NZ * NY)
SHARE = FEATURES // (NX * NC)
COLS = FEATURES // (NZ * NY)
F32 = jnp.float32
BF16 = jnp.bfloat16

SMEM = pl.BlockSpec(memory_space=pltpu.SMEM)
VMEM = pl.BlockSpec(memory_space=pltpu.VMEM)


def params(mib):
    return pltpu.CompilerParams(vmem_limit_bytes=mib * 1024 * 1024)


def cost(macs, nbytes):
    return pl.CostEstimate(flops=2 * macs, bytes_accessed=nbytes, transcendentals=0)


TN = (((0,), (0,)), ((), ()))
NT = (((1,), (1,)), ((), ()))
HALF = TOK // 2
ANY = pl.BlockSpec(memory_space=pl.ANY)


def whole(shape):
    return pl.BlockSpec(shape, lambda i: (0,) * len(shape))


def lead(shape):
    return pl.BlockSpec(shape, lambda i: (i,) + (0,) * (len(shape) - 1))


def cotangent_kernel(idx, *refs):
    pieces, (weight, dy, gram, back, held, down, sems, down_sem, out_sem) = refs[:NY], refs[NY:]
    y = idx[1]

    def incoming(j):
        return pltpu.make_async_copy(pieces[j], held.at[:, lax.rem(y - j + NY, NY)], sems.at[j])

    fetch = pltpu.make_async_copy(weight.at[:, 2], down, down_sem)
    for j in range(NY):
        incoming(j).start()
    fetch.start()
    for j in range(NY):
        incoming(j).wait()
    keep = pltpu.make_async_copy(held, dy, out_sem)
    keep.start()
    for h in range(2):

        def step(z, acc):
            block = held[z, :, :, h * HALF : (h + 1) * HALF].reshape(SHARE, HALF)
            return acc + lax.dot_general(block, block, TN, preferred_element_type=F32)

        gram[h] = lax.fori_loop(0, NZ, step, jnp.zeros((HALF, HALF), F32))
    fetch.wait()
    back[...] = jnp.zeros_like(back)

    def share(d, carry):
        back[...] += jnp.dot(down[d], held[d].reshape(SHARE, TOK), preferred_element_type=F32)
        return carry

    lax.fori_loop(0, NX * NC, share, 0)
    keep.wait()


def cotangent_call(idx, pieces, weight):
    return pl.pallas_call(
        cotangent_kernel,
        out_shape=(
            jax.ShapeDtypeStruct((NZ, NY, COLS, TOK), BF16),
            jax.ShapeDtypeStruct((2, HALF, HALF), F32),
            jax.ShapeDtypeStruct((UNITS, TOK), F32),
        ),
        in_specs=[SMEM] + [ANY] * (NY + 1),
        out_specs=(ANY, VMEM, VMEM),
        scratch_shapes=[
            pltpu.VMEM((NZ, NY, COLS, TOK), BF16),
            pltpu.VMEM((NX * NC, UNITS, SHARE), BF16),
            pltpu.SemaphoreType.DMA((NY,)),
            pltpu.SemaphoreType.DMA,
            pltpu.SemaphoreType.DMA,
        ],
        compiler_params=params(60),
        cost_estimate=cost((UNITS + HALF) * TOK * FEATURES, 11 << 20),
        name="cotangent",
    )(idx, *pieces, weight)


def hidden_kernel(idx, *refs):
    pieces, (weight, gain, dy_gram, back, xs, hidden, inverse, down_sq, grads) = refs[:NZ], refs[NZ : NZ + 9]
    x, held, acc, sems, weight_sems, out_sems = refs[NZ + 9 :]
    z, y = idx[0], idx[1]

    def place(j):
        return lax.rem(z - j + NZ, NZ)

    def fetch(j):
        d = place(j)
        return pltpu.make_async_copy(weight.at[d, :2], held.at[d], weight_sems.at[j])

    def keep(j):
        d = place(j)
        return pltpu.make_async_copy(x.at[d], xs.at[d], out_sems.at[j])

    for j in range(NZ):
        for i in range(NY):
            slot = lax.rem(y - i + NY, NY)
            pltpu.make_async_copy(pieces[j].at[i], x.at[place(j), slot], sems.at[j]).start()
        fetch(j).start()
    acc[...] = jnp.zeros_like(acc)

    def share(j, total):
        d = place(j)
        pltpu.make_async_copy(pieces[0], x.at[d], sems.at[j]).wait()
        fetch(j).wait()
        keep(j).start()
        row = gain[pl.ds(d, 1), :]
        block = x[d].reshape(SHARE, TOK)
        for k in range(2):
            scaled = (held[d, k].astype(F32) * row).astype(BF16)
            acc[k] += jnp.dot(scaled, block, preferred_element_type=F32)
        for i in range(NY):
            wide = x[d, i].astype(F32)
            total += jnp.sum((wide * wide).reshape(COLS // 8, 8, TOK), axis=0)
        return total

    total = lax.fori_loop(0, NZ, share, jnp.zeros((8, TOK), F32))
    mean = jnp.sum(total, axis=0, keepdims=True) * (1.0 / FEATURES)
    inverse[...] = lax.rsqrt(mean + 1e-05)

    def rows(i, carry):
        r = pl.ds(pl.multiple_of(i * 32, 32), 32)
        inv = inverse[...]
        g = acc[0, r, :] * inv
        u = acc[1, r, :] * inv
        b = back[r, :]
        sigma = jax.nn.sigmoid(g)
        swish = g * sigma
        hidden[r, :] = (swish * u).astype(BF16)
        grads[0, r, :] = (b * u * sigma * (1.0 + g * (1.0 - sigma))).astype(BF16)
        grads[1, r, :] = (b * swish).astype(BF16)
        return carry

    lax.fori_loop(0, UNITS // 32, rows, 0)
    for h in range(2):
        own = hidden[:, h * HALF : (h + 1) * HALF]
        pairs = lax.dot_general(own, own, TN, preferred_element_type=F32) * dy_gram[h]
        for s in range(HALF // SEQ):
            part = pairs[s * SEQ : (s + 1) * SEQ, s * SEQ : (s + 1) * SEQ]
            value = jnp.sum(jnp.sum(part, axis=0, keepdims=True), axis=1, keepdims=True)
            i = h * (HALF // SEQ) + s
            down_sq[:, i : i + 1, :] = jnp.broadcast_to(value.reshape(1, 1, 1), (NY, 1, 128))

    def drain(j, carry):
        keep(j).wait()
        return carry

    lax.fori_loop(0, NZ, drain, 0)


def hidden_call(idx, pieces, weight, gain, dy_gram, back):
    return pl.pallas_call(
        hidden_kernel,
        out_shape=(
            jax.ShapeDtypeStruct((NZ, NY, COLS, TOK), BF16),
            jax.ShapeDtypeStruct((UNITS, TOK), BF16),
            jax.ShapeDtypeStruct((1, TOK), F32),
            jax.ShapeDtypeStruct((NY, LOCAL, 128), F32),
            jax.ShapeDtypeStruct((2, UNITS, TOK), BF16),
        ),
        in_specs=[SMEM] + [ANY] * (NZ + 1) + [VMEM] * 3,
        out_specs=(ANY,) + (VMEM,) * 4,
        scratch_shapes=[
            pltpu.VMEM((NZ, NY, COLS, TOK), BF16),
            pltpu.VMEM((NX * NC, 2, UNITS, SHARE), BF16),
            pltpu.VMEM((2, UNITS, TOK), F32),
            pltpu.SemaphoreType.DMA((NZ,)),
            pltpu.SemaphoreType.DMA((NZ,)),
            pltpu.SemaphoreType.DMA((NZ,)),
        ],
        compiler_params=params(60),
        cost_estimate=cost(2 * UNITS * TOK * FEATURES, 14 << 20),
        name="hidden",
    )(idx, *pieces, weight, gain, dy_gram, back)


def gain_kernel(grads, inverse, xs, weight, out):
    token = lax.broadcasted_iota(jnp.int32, (TOK, 128), 0)
    column = lax.broadcasted_iota(jnp.int32, (TOK, 128), 1)
    select = jnp.where(token // SEQ == column, 1.0, 0.0).astype(BF16)
    parts, wide = 2, SHARE // 2
    for d in range(2):
        for h in range(parts):
            f = slice(h * wide, (h + 1) * wide)
            normed = lax.dot_general(weight[d, 0, :, f], grads[0], TN, preferred_element_type=F32)
            normed += lax.dot_general(weight[d, 1, :, f], grads[1], TN, preferred_element_type=F32)
            group = wide // COLS
            block = xs[d, h * group : (h + 1) * group].reshape(wide, TOK)
            product = block.astype(F32) * inverse[...] * normed
            high = product.astype(BF16)
            low = (product - high.astype(F32)).astype(BF16)
            total = jnp.dot(high, select, preferred_element_type=F32)
            total += jnp.dot(low, select, preferred_element_type=F32)
            flat = total.T[:LOCAL]
            for k in range(wide // 128):
                tile = h * (wide // 128) + k
                out[d, tile * LOCAL : (tile + 1) * LOCAL, :] = flat[:, k * 128 : (k + 1) * 128]


def gain_call(grads, inverse, xs, weight):
    return pl.pallas_call(
        gain_kernel,
        grid=(NZ // 2,),
        out_shape=jax.ShapeDtypeStruct((NZ, SHARE // 128 * LOCAL, 128), F32),
        in_specs=[
            whole((2, UNITS, TOK)),
            whole((1, TOK)),
            lead((2, NY, COLS, TOK)),
            lead((2, 2, UNITS, SHARE)),
        ],
        out_specs=lead((2, SHARE // 128 * LOCAL, 128)),
        compiler_params=params(60),
        cost_estimate=cost(3 * UNITS * TOK * FEATURES, 9 << 20),
        name="gain_term",
    )(grads, inverse, xs, weight)


def join_kernel(part, gain_part, out):
    total = jnp.sum(part[...], axis=0, keepdims=True)
    out[:, :LOCAL, :] = jnp.broadcast_to(total, (NZ, LOCAL, 128))
    out[:, LOCAL:, :] = gain_part[...]


def join_call(part, gain_part):
    rows = LOCAL + gain_part.shape[1]
    return pl.pallas_call(
        join_kernel,
        out_shape=jax.ShapeDtypeStruct((NZ, rows, 128), F32),
        in_specs=[VMEM, VMEM],
        out_specs=VMEM,
        compiler_params=params(60),
        name="join_parts",
    )(part, gain_part)


def gain_sq_kernel(idx, part, out):
    y = idx[1]
    gain = jnp.sum(part[...], axis=0).reshape(SHARE // 128, LOCAL, 128)
    rows = jnp.sum(gain * gain, axis=0)
    value = jnp.broadcast_to(jnp.sum(rows, axis=1, keepdims=True), (LOCAL, COLS))
    mine = jnp.zeros((LOCAL, COLS), F32)
    for k in range(NY):
        lanes = gain[k // 2, :, k % 2 * COLS : (k % 2 + 1) * COLS]
        mine = jnp.where(y == k, lanes, mine)
    out[...] = jnp.broadcast_to(jnp.concatenate([mine, value], axis=1)[None], out.shape)


def gain_scale_kernel(idx, part, out):
    bound = 0.5 * math.sqrt(SEQ * FEATURES)
    total = jnp.zeros((1, COLS), F32)
    for g in range(NX * NC):
        group = part[g * NZ : (g + 1) * NZ]
        square = jnp.sum(group, axis=0)[:, COLS:]
        scale = jnp.minimum(1.0, bound / (jnp.sqrt(square) + 1e-06)) / SEQS
        total += jnp.sum(scale * part[g * NZ + idx[0]][:, :COLS], axis=0, keepdims=True)
    out[...] = total


def grad_kernel(part, hidden, dy, out, added, scaled):
    @pl.when(pl.program_id(0) == 0)
    def _():
        bound = 0.6 * math.sqrt(SEQ * FF * FEATURES)
        total = jnp.sum(part[:, :LOCAL, :], axis=0)
        scale = jnp.minimum(1.0, bound / (jnp.sqrt(total) + 1e-06)) / SEQS
        first = lax.broadcasted_iota(jnp.int32, (1, 128), 1) < SEQ
        row = jnp.concatenate(
            [jnp.where(first, scale[2 * k : 2 * k + 1], scale[2 * k + 1 : 2 * k + 2]) for k in range(LOCAL // 2)],
            axis=1,
        )
        scaled[...] = (hidden[...].astype(F32) * row).astype(BF16)
        gain = jnp.sum(part[:, LOCAL:, :], axis=0, keepdims=True)
        added[...] = jnp.broadcast_to(gain, added.shape)

    for d in range(2):
        block = dy[d].reshape(SHARE, TOK)
        out[d] = lax.dot_general(scaled[...], block, NT, preferred_element_type=F32).astype(BF16)


def grad_call(part, hidden, dy):
    gain_shape = (NY, part.shape[1] - LOCAL, 128)
    return pl.pallas_call(
        grad_kernel,
        grid=(NZ // 2,),
        out_shape=(
            jax.ShapeDtypeStruct((NX * NC, UNITS, SHARE), BF16),
            jax.ShapeDtypeStruct(gain_shape, F32),
        ),
        in_specs=[whole(part.shape), whole((UNITS, TOK)), lead((2, NY, COLS, TOK))],
        out_specs=(lead((2, UNITS, SHARE)), whole(gain_shape)),
        scratch_shapes=[pltpu.VMEM((UNITS, TOK), BF16)],
        compiler_params=params(60),
        cost_estimate=cost(UNITS * TOK * FEATURES, 6 << 20),
        name="grad_down",
    )(part, hidden, dy)


def spread(block, axis, count):
    return lax.all_to_all(
        jnp.broadcast_to(block[None], (count,) + block.shape), axis, split_axis=0, concat_axis=0, tiled=True
    )


def exchange(blocks, axis):
    return lax.all_to_all(blocks, axis, split_axis=0, concat_axis=0, tiled=True)


def ring(block, axis, size):
    turn = lambda part, k: lax.ppermute(part, axis, [(i, (i + k) % size) for i in range(size)])
    up, down = [block], [block]
    for step in range(size // 2):
        up.append(turn(up[-1], 1))
        if step < size // 2 - 1:
            down.append(turn(down[-1], -1))
    return up + down[:0:-1]


def body(tokens, gain, cotangent, gate_weight, up_weight, down_weight):
    idx = jnp.stack([lax.axis_index("z"), lax.axis_index("y")]).astype(jnp.int32)
    dp = ("x", "core")
    weight = lax.all_gather(jnp.stack([gate_weight.T, up_weight.T, down_weight]), dp, axis=0)
    dy_pieces = ring(spread(cotangent.T, "z", NZ), "y", NY)
    pieces = ring(jnp.stack(ring(tokens.T, "y", NY)), "z", NZ)

    dy, dy_gram, back = cotangent_call(idx, dy_pieces, weight)
    xs, hidden, inverse, sq_part, grads = hidden_call(
        idx, pieces, weight, gain.reshape(NX * NC, SHARE), dy_gram, back
    )
    part = exchange(sq_part, "y")
    grads, sq_part = lax.optimization_barrier((grads, sq_part))
    gain_part = gain_call(grads, inverse, xs, weight)
    part = exchange(join_call(part, gain_part), "z")
    terms, added = grad_call(part, hidden, dy)
    grad_down = lax.psum_scatter(terms, dp, scatter_dimension=0).astype(F32)

    everyone = ("x", "core", "z")
    message = pl.pallas_call(
        gain_sq_kernel,
        out_shape=jax.ShapeDtypeStruct((NX * NC * NZ, LOCAL, 128), F32),
        in_specs=[SMEM, VMEM],
        out_specs=VMEM,
        compiler_params=params(60),
        name="gain_sq",
    )(idx, exchange(added, "y"))
    grad_gain = pl.pallas_call(
        gain_scale_kernel,
        out_shape=jax.ShapeDtypeStruct((1, COLS), F32),
        in_specs=[SMEM, VMEM],
        out_specs=VMEM,
        compiler_params=params(60),
        name="grad_gain",
    )(idx, exchange(message, everyone)).reshape(COLS)
    return (grad_down, grad_gain)


def solution(mesh):
    split = Mesh(mesh.devices.reshape(NX, NC, NZ, NY), ("x", "core", "z", "y"))
    dp, tensor = ("x", "core"), ("z", "y")
    in_specs = (P(dp, tensor), P(), P(dp, tensor), P(dp, tensor), P(dp, tensor), P(tensor, dp))
    out_specs = (P(tensor, dp), P(tensor))
    return jax.shard_map(body, mesh=split, in_specs=in_specs, out_specs=out_specs, check_vma=False)
```

```python
import math

import jax
import jax.numpy as jnp
from jax import lax
from jax.experimental import pallas as pl
from jax.experimental.pallas import tpu as pltpu
from jax.sharding import Mesh
from jax.sharding import PartitionSpec as P

FEATURES = 4096
FF = 14336
SEQ = 64
SEQS = 64
NX, NC, NZ, NY = 4, 2, 8, 8
LOCAL = 8
TOK = LOCAL * SEQ
UNITS = FF // (NZ * NY)
SHARE = FEATURES // (NX * NC)
COLS = FEATURES // (NZ * NY)
F32 = jnp.float32
BF16 = jnp.bfloat16

SMEM = pl.BlockSpec(memory_space=pltpu.SMEM)
VMEM = pl.BlockSpec(memory_space=pltpu.VMEM)


def params(mib):
    return pltpu.CompilerParams(vmem_limit_bytes=mib * 1024 * 1024)


def cost(macs, nbytes):
    return pl.CostEstimate(flops=2 * macs, bytes_accessed=nbytes, transcendentals=0)


TN = (((0,), (0,)), ((), ()))
NT = (((1,), (1,)), ((), ()))
HALF = TOK // 2
ANY = pl.BlockSpec(memory_space=pl.ANY)


def whole(shape):
    return pl.BlockSpec(shape, lambda i: (0,) * len(shape))


def lead(shape):
    return pl.BlockSpec(shape, lambda i: (i,) + (0,) * (len(shape) - 1))


def cotangent_kernel(idx, *refs):
    pieces, (weight, dy, gram, back, held, down, sems, down_sem, out_sem) = refs[:NY], refs[NY:]
    y = idx[1]

    def incoming(j):
        return pltpu.make_async_copy(pieces[j], held.at[:, lax.rem(y - j + NY, NY)], sems.at[j])

    fetch = pltpu.make_async_copy(weight.at[:, 2], down, down_sem)
    for j in range(NY):
        incoming(j).start()
    fetch.start()
    for j in range(NY):
        incoming(j).wait()
    keep = pltpu.make_async_copy(held, dy, out_sem)
    keep.start()
    for h in range(2):

        def step(z, acc):
            block = held[z, :, :, h * HALF : (h + 1) * HALF].reshape(SHARE, HALF)
            return acc + lax.dot_general(block, block, TN, preferred_element_type=F32)

        gram[h] = lax.fori_loop(0, NZ, step, jnp.zeros((HALF, HALF), F32))
    fetch.wait()
    back[...] = jnp.zeros_like(back)

    def share(d, carry):
        back[...] += jnp.dot(down[d], held[d].reshape(SHARE, TOK), preferred_element_type=F32)
        return carry

    lax.fori_loop(0, NX * NC, share, 0)
    keep.wait()


def cotangent_call(idx, pieces, weight):
    return pl.pallas_call(
        cotangent_kernel,
        out_shape=(
            jax.ShapeDtypeStruct((NZ, NY, COLS, TOK), BF16),
            jax.ShapeDtypeStruct((2, HALF, HALF), F32),
            jax.ShapeDtypeStruct((UNITS, TOK), F32),
        ),
        in_specs=[SMEM] + [ANY] * (NY + 1),
        out_specs=(ANY, VMEM, VMEM),
        scratch_shapes=[
            pltpu.VMEM((NZ, NY, COLS, TOK), BF16),
            pltpu.VMEM((NX * NC, UNITS, SHARE), BF16),
            pltpu.SemaphoreType.DMA((NY,)),
            pltpu.SemaphoreType.DMA,
            pltpu.SemaphoreType.DMA,
        ],
        compiler_params=params(60),
        cost_estimate=cost((UNITS + HALF) * TOK * FEATURES, 11 << 20),
        name="cotangent",
    )(idx, *pieces, weight)


def hidden_kernel(idx, *refs):
    pieces, (weight, gain, dy_gram, back, xs, hidden, inverse, down_sq, grads) = refs[:NZ], refs[NZ : NZ + 9]
    x, held, acc, sems, weight_sems, out_sems = refs[NZ + 9 :]
    z, y = idx[0], idx[1]

    def place(j):
        return lax.rem(z - j + NZ, NZ)

    def fetch(j):
        d = place(j)
        return pltpu.make_async_copy(weight.at[d, :2], held.at[d], weight_sems.at[j])

    def keep(j):
        d = place(j)
        return pltpu.make_async_copy(x.at[d], xs.at[d], out_sems.at[j])

    for j in range(NZ):
        for i in range(NY):
            slot = lax.rem(y - i + NY, NY)
            pltpu.make_async_copy(pieces[j].at[i], x.at[place(j), slot], sems.at[j]).start()
        fetch(j).start()
    acc[...] = jnp.zeros_like(acc)

    def share(j, total):
        d = place(j)
        pltpu.make_async_copy(pieces[0], x.at[d], sems.at[j]).wait()
        fetch(j).wait()
        keep(j).start()
        row = gain[pl.ds(d, 1), :]
        block = x[d].reshape(SHARE, TOK)
        for k in range(2):
            scaled = (held[d, k].astype(F32) * row).astype(BF16)
            acc[k] += jnp.dot(scaled, block, preferred_element_type=F32)
        for i in range(NY):
            wide = x[d, i].astype(F32)
            total += jnp.sum((wide * wide).reshape(COLS // 8, 8, TOK), axis=0)
        return total

    total = lax.fori_loop(0, NZ, share, jnp.zeros((8, TOK), F32))
    mean = jnp.sum(total, axis=0, keepdims=True) * (1.0 / FEATURES)
    inverse[...] = lax.rsqrt(mean + 1e-05)

    def rows(i, carry):
        r = pl.ds(pl.multiple_of(i * 32, 32), 32)
        inv = inverse[...]
        g = acc[0, r, :] * inv
        u = acc[1, r, :] * inv
        b = back[r, :]
        sigma = jax.nn.sigmoid(g)
        swish = g * sigma
        hidden[r, :] = (swish * u).astype(BF16)
        grads[0, r, :] = (b * u * sigma * (1.0 + g * (1.0 - sigma))).astype(BF16)
        grads[1, r, :] = (b * swish).astype(BF16)
        return carry

    lax.fori_loop(0, UNITS // 32, rows, 0)
    for h in range(2):
        own = hidden[:, h * HALF : (h + 1) * HALF]
        pairs = lax.dot_general(own, own, TN, preferred_element_type=F32) * dy_gram[h]
        for s in range(HALF // SEQ):
            part = pairs[s * SEQ : (s + 1) * SEQ, s * SEQ : (s + 1) * SEQ]
            value = jnp.sum(jnp.sum(part, axis=0, keepdims=True), axis=1, keepdims=True)
            i = h * (HALF // SEQ) + s
            down_sq[i : i + 1, :] = jnp.broadcast_to(value, (1, 128))

    def drain(j, carry):
        keep(j).wait()
        return carry

    lax.fori_loop(0, NZ, drain, 0)


def hidden_call(idx, pieces, weight, gain, dy_gram, back):
    return pl.pallas_call(
        hidden_kernel,
        out_shape=(
            jax.ShapeDtypeStruct((NZ, NY, COLS, TOK), BF16),
            jax.ShapeDtypeStruct((UNITS, TOK), BF16),
            jax.ShapeDtypeStruct((1, TOK), F32),
            jax.ShapeDtypeStruct((LOCAL, 128), F32),
            jax.ShapeDtypeStruct((2, UNITS, TOK), BF16),
        ),
        in_specs=[SMEM] + [ANY] * (NZ + 1) + [VMEM] * 3,
        out_specs=(ANY,) + (VMEM,) * 4,
        scratch_shapes=[
            pltpu.VMEM((NZ, NY, COLS, TOK), BF16),
            pltpu.VMEM((NX * NC, 2, UNITS, SHARE), BF16),
            pltpu.VMEM((2, UNITS, TOK), F32),
            pltpu.SemaphoreType.DMA((NZ,)),
            pltpu.SemaphoreType.DMA((NZ,)),
            pltpu.SemaphoreType.DMA((NZ,)),
        ],
        compiler_params=params(60),
        cost_estimate=cost(2 * UNITS * TOK * FEATURES, 14 << 20),
        name="hidden",
    )(idx, *pieces, weight, gain, dy_gram, back)


def gain_kernel(grads, inverse, xs, weight, down_sq, out):
    token = lax.broadcasted_iota(jnp.int32, (TOK, 128), 0)
    column = lax.broadcasted_iota(jnp.int32, (TOK, 128), 1)
    select = jnp.where(token // SEQ == column, 1.0, 0.0).astype(BF16)
    parts, wide = 2, SHARE // 2
    for d in range(2):
        for h in range(parts):
            f = slice(h * wide, (h + 1) * wide)
            normed = lax.dot_general(weight[d, 0, :, f], grads[0], TN, preferred_element_type=F32)
            normed += lax.dot_general(weight[d, 1, :, f], grads[1], TN, preferred_element_type=F32)
            group = wide // COLS
            block = xs[d, h * group : (h + 1) * group].reshape(wide, TOK)
            product = block.astype(F32) * inverse[...] * normed
            high = product.astype(BF16)
            low = (product - high.astype(F32)).astype(BF16)
            total = jnp.dot(high, select, preferred_element_type=F32)
            total += jnp.dot(low, select, preferred_element_type=F32)
            flat = total.T[:LOCAL]
            for k in range(group):
                lanes = flat[:, k * COLS : (k + 1) * COLS]
                out[d * NY + h * group + k] = jnp.concatenate([lanes, down_sq[:, :COLS]], axis=1)


def gain_call(grads, inverse, xs, weight, down_sq):
    return pl.pallas_call(
        gain_kernel,
        grid=(NZ // 2,),
        out_shape=jax.ShapeDtypeStruct((NZ * NY, LOCAL, 128), F32),
        in_specs=[
            whole((2, UNITS, TOK)),
            whole((1, TOK)),
            lead((2, NY, COLS, TOK)),
            lead((2, 2, UNITS, SHARE)),
            whole((LOCAL, 128)),
        ],
        out_specs=lead((2 * NY, LOCAL, 128)),
        compiler_params=params(60),
        cost_estimate=cost(3 * UNITS * TOK * FEATURES, 9 << 20),
        name="gain_term",
    )(grads, inverse, xs, weight, down_sq)


def gain_scale_kernel(part, gain, out):
    square = jnp.sum(part[...], axis=0)
    bound = 0.5 * math.sqrt(SEQ * FEATURES)
    scale = jnp.minimum(1.0, bound / (jnp.sqrt(square) + 1e-06)) / SEQS
    value = jnp.sum(scale * gain[...], axis=0, keepdims=True)
    out[...] = jnp.broadcast_to(value[None], out.shape)


def grad_kernel(part, hidden, dy, out, gain, square, scaled):
    @pl.when(pl.program_id(0) == 0)
    def _():
        bound = 0.6 * math.sqrt(SEQ * FF * FEATURES)
        sums = jnp.sum(part[...], axis=0)
        gain[...] = sums
        own = sums[:, :COLS]
        squares = jnp.sum(own * own, axis=1, keepdims=True)
        square[...] = jnp.broadcast_to(squares[None], square.shape)
        total = jnp.broadcast_to(sums[:, COLS : COLS + 1], (LOCAL, 128))
        scale = jnp.minimum(1.0, bound / (jnp.sqrt(total) + 1e-06)) / SEQS
        first = lax.broadcasted_iota(jnp.int32, (1, 128), 1) < SEQ
        row = jnp.concatenate(
            [jnp.where(first, scale[2 * k : 2 * k + 1], scale[2 * k + 1 : 2 * k + 2]) for k in range(LOCAL // 2)],
            axis=1,
        )
        scaled[...] = (hidden[...].astype(F32) * row).astype(BF16)

    for d in range(2):
        block = dy[d].reshape(SHARE, TOK)
        out[d] = lax.dot_general(scaled[...], block, NT, preferred_element_type=F32).astype(BF16)


def grad_call(part, hidden, dy):
    return pl.pallas_call(
        grad_kernel,
        grid=(NZ // 2,),
        out_shape=(
            jax.ShapeDtypeStruct((NX * NC, UNITS, SHARE), BF16),
            jax.ShapeDtypeStruct((LOCAL, 128), F32),
            jax.ShapeDtypeStruct(part.shape, F32),
        ),
        in_specs=[whole(part.shape), whole((UNITS, TOK)), lead((2, NY, COLS, TOK))],
        out_specs=(lead((2, UNITS, SHARE)), whole((LOCAL, 128)), whole(part.shape)),
        scratch_shapes=[pltpu.VMEM((UNITS, TOK), BF16)],
        compiler_params=params(60),
        cost_estimate=cost(UNITS * TOK * FEATURES, 6 << 20),
        name="grad_down",
    )(part, hidden, dy)


def spread(block, axis, count):
    return lax.all_to_all(
        jnp.broadcast_to(block[None], (count,) + block.shape), axis, split_axis=0, concat_axis=0, tiled=True
    )


def exchange(blocks, axis):
    return lax.all_to_all(blocks, axis, split_axis=0, concat_axis=0, tiled=True)


def ring(block, axis, size):
    turn = lambda part, k: lax.ppermute(part, axis, [(i, (i + k) % size) for i in range(size)])
    up, down = [block], [block]
    for step in range(size // 2):
        up.append(turn(up[-1], 1))
        if step < size // 2 - 1:
            down.append(turn(down[-1], -1))
    return up + down[:0:-1]


def body(tokens, gain, cotangent, gate_weight, up_weight, down_weight):
    idx = jnp.stack([lax.axis_index("z"), lax.axis_index("y")]).astype(jnp.int32)
    dp = ("x", "core")
    weight = lax.all_gather(jnp.stack([gate_weight.T, up_weight.T, down_weight]), dp, axis=0)
    dy_pieces = ring(spread(cotangent.T, "z", NZ), "y", NY)
    pieces = ring(jnp.stack(ring(tokens.T, "y", NY)), "z", NZ)

    dy, dy_gram, back = cotangent_call(idx, dy_pieces, weight)
    xs, hidden, inverse, sq_part, grads = hidden_call(
        idx, pieces, weight, gain.reshape(NX * NC, SHARE), dy_gram, back
    )
    tensor = ("z", "y")
    part = exchange(gain_call(grads, inverse, xs, weight, sq_part), tensor)
    terms, gain_mine, square = grad_call(part, hidden, dy)
    grad_down = lax.psum_scatter(terms, dp, scatter_dimension=0).astype(F32)
    gain_local = pl.pallas_call(
        gain_scale_kernel,
        out_shape=jax.ShapeDtypeStruct((NX * NC, 8, 128), F32),
        in_specs=[VMEM, VMEM],
        out_specs=VMEM,
        compiler_params=params(60),
        name="gain_scale",
    )(exchange(square, tensor), gain_mine)
    grad_gain = jnp.sum(exchange(gain_local, dp)[:, 0, :COLS], axis=0)
    return (grad_down, grad_gain)


def solution(mesh):
    split = Mesh(mesh.devices.reshape(NX, NC, NZ, NY), ("x", "core", "z", "y"))
    dp, tensor = ("x", "core"), ("z", "y")
    in_specs = (P(dp, tensor), P(), P(dp, tensor), P(dp, tensor), P(dp, tensor), P(tensor, dp))
    out_specs = (P(tensor, dp), P(tensor))
    return jax.shard_map(body, mesh=split, in_specs=in_specs, out_specs=out_specs, check_vma=False)
```
